256 devices in a mesh: context: 16 (over y, x), tensor: 16 (over z, core).
Axes of the slice: x: 4, y: 4, z: 8, core: 2. Of those that a mesh axis runs over, the one named last changes fastest.
Arguments:
- x_in: bfloat16 [4096, 8192], P('context', 'tensor'), may hold values from -6 to 6
- gate_in: bfloat16 [4096, 8192], P('context', 'tensor'), may hold values from -12 to 12
- b_in: bfloat16 [4096, 1024], P('context'), may hold values from -0.375 to 0.375
- c_in: bfloat16 [4096, 1024], P('context'), may hold values from -6 to 6
- dt_raw: float32 [128, 4096], P('tensor', 'context'), may hold values from -5 to 5
- dt_bias: float32 [128], P('tensor'), may hold values from -3 to -1
- a_log: float32 [128], P('tensor'), as said below
- skip_weight: float32 [128], P('tensor'), may hold values from 0.5 to 1.5
- norm_gain: float32 [8192], P('tensor'), may hold values from 0.5 to 1.5
- w_out: bfloat16 [8192, 8192], P('tensor'), may hold values from -0.0625 to 0.0625
- doc_starts: int32 [4], replicated, may hold values from 1 to 3968, as said below
- grad_out: bfloat16 [4096, 8192], P(('context', 'tensor')), may hold values from -6 to 6
Outputs:
- mixed_out: bfloat16 [4096, 8192], P(('context', 'tensor'))
- grad_x: bfloat16 [4096, 8192], P('context', 'tensor')
- grad_gate: bfloat16 [4096, 8192], P('context', 'tensor')
- grad_b: bfloat16 [4096, 1024], P('context', 'tensor')
- grad_c: bfloat16 [4096, 1024], P('context', 'tensor')
- grad_dt: float32 [128, 4096], P('tensor', 'context')
The draws below stay inside these ranges and needn't reach their ends.
Inputs may be any that keep to these rules, and one draw needn't show every extreme that they name: `doc_starts`: 4 distinct positions in increasing order, the last of them 4096 - 256 / 2; position 0 begins a document as well. exp(a_log) lies between 0.2 / 4096 and 0.5.
All inputs are finite; a program needn't handle non-finite values.
Results may differ from the reference program's by a relative error of at most 0.0049.
Values may be sent and summed in bfloat16 or wider, within the bound.
A program may use at most 128 MiB of HBM per device.

```python
import math
import jax
import jax.numpy as jnp
from jax import lax

D = 8192
HEAD_DIM = 64
STATE = 256
BLOCK = 256
NDOCS = 4
GROUP_HEADS = 32
HEADS = 128
GROUPS = 4
INNER = 8192
TOKENS = 4096


def draw_a_log(key, part):
    key = jax.random.fold_in(key, 7)
    bottom = math.log(1.0 / TOKENS)
    ceiling = math.log(0.5)
    return jax.random.uniform(key, (HEADS,), jnp.float32, bottom, ceiling)


def scaled_gates(base, lowest, ratio):
    channels = GROUP_HEADS * HEAD_DIM
    position = (jnp.arange(INNER, dtype=jnp.int32) % channels).astype(jnp.float32)
    scale = lowest * ratio ** (position / (channels - 1))
    return (base * scale[None, :]).astype(jnp.bfloat16)


def draw_gate_in(key, part):
    key = jax.random.fold_in(key, 5)
    base = jnp.clip(jax.random.normal(key, (TOKENS, INNER), jnp.float32), -6.0, 6.0)
    return scaled_gates(base, 0.5, 4.0)


def draw_doc_starts(key, part):
    key = jax.random.fold_in(key, 11)
    last_start = TOKENS - BLOCK // 2
    picked = jax.random.permutation(key, last_start - 1)[:NDOCS - 1] + 1
    whole = jnp.concatenate([picked.astype(jnp.int32), jnp.full((1,), last_start, jnp.int32)])
    return jnp.sort(whole).astype(jnp.int32)


def level_of(own_key, shape, cuts, smallest, top_value):
    level = 1.0
    for dim, parts in cuts:
        heights = jax.random.uniform(jax.random.fold_in(jax.random.fold_in(own_key, 6), dim), (parts,), jnp.float32, smallest / len(cuts), top_value / len(cuts))
        level = level * jnp.repeat(jnp.exp(heights), shape[dim] // parts).reshape((-1,) + (1,) * (len(shape) - 1 - dim))
    return level


def bell_draw(rng, extent, scale, limit, split=(), held_as=jnp.bfloat16):
    array = jax.random.normal(rng, extent, jnp.float32) * scale
    if len(split) > 0:
        array = level_of(rng, extent, split, -0.22, 0.18) * array
    return jnp.clip(array, min=-limit, max=limit).astype(held_as)


def setup_inputs(seed: int = 0) -> dict:
    key_list = jax.random.split(jax.random.key(seed), 13)
    x_in = bell_draw(key_list[0], (TOKENS, INNER), 1.0, 6.0, ((0, 16), (1, 16)))
    gate_in = draw_gate_in(jax.random.fold_in(key_list[12], 71), 0)
    b_in = bell_draw(key_list[2], (TOKENS, GROUPS * STATE), (STATE ** -0.5), 0.375, ((0, 16),))
    c_in = bell_draw(key_list[3], (TOKENS, GROUPS * STATE), 1.0, 6.0, ((0, 16),))
    dt_raw = bell_draw(key_list[4], (HEADS, TOKENS), 1.0, 5.0, ((0, 16), (1, 16)), jnp.float32)
    dt_bias = jnp.clip(-3.0 + 2.0 * jax.random.uniform(key_list[5], (HEADS,), jnp.float32) ** level_of(key_list[5], (HEADS,), ((0, 16),), -0.2, 0.2), -3.0, -1.0)
    a_log = draw_a_log(jax.random.fold_in(key_list[12], 71), 0)
    skip_weight = jnp.clip(0.5 + 1.0 * jax.random.uniform(key_list[7], (HEADS,), jnp.float32) ** level_of(key_list[7], (HEADS,), ((0, 16),), -0.2, 0.2), 0.5, 1.5)
    norm_gain = jnp.clip(1.0 + 0.1 * jax.random.normal(key_list[8], (INNER,), jnp.float32), 0.5, 1.5)
    w_out = bell_draw(key_list[9], (INNER, D), INNER ** -0.5, 0.0625, ((0, 16),))
    doc_starts = draw_doc_starts(jax.random.fold_in(key_list[12], 71), 0)
    grad_out = bell_draw(key_list[11], (TOKENS, D), 1.0, 6.0, ((0, 256),))
    return dict(x_in=x_in, gate_in=gate_in, b_in=b_in, c_in=c_in, dt_raw=dt_raw, dt_bias=dt_bias, a_log=a_log, skip_weight=skip_weight, norm_gain=norm_gain, w_out=w_out, doc_starts=doc_starts, grad_out=grad_out)


exact_prec = lax.Precision.HIGHEST
norm_epsilon = 1e-05

def ssd_forward(x_f, gate_f, b_f, c_f, dt_f, dt_bias, a_log, skip_weight, norm_gain, resets):
    tokens = x_f.shape[0]
    groups = b_f.shape[1] // STATE
    per_group = GROUP_HEADS
    count = tokens // BLOCK
    x_groups = x_f.reshape(tokens, groups, per_group, HEAD_DIM)
    step = jax.nn.softplus(dt_f + dt_bias[:, None])
    rate = step * (-jnp.exp(a_log))[:, None]
    step_blocks = step.reshape(groups, per_group, count, BLOCK).transpose(2, 0, 1, 3)
    rate_blocks = rate.reshape(groups, per_group, count, BLOCK).transpose(2, 0, 1, 3)
    x_blocks = x_groups.reshape(count, BLOCK, groups, per_group, HEAD_DIM)
    b_blocks = b_f.reshape(count, BLOCK, groups, STATE)
    c_blocks = c_f.reshape(count, BLOCK, groups, STATE)
    reset_blocks = resets.reshape(count, BLOCK)
    places = jnp.arange(BLOCK)
    lower_tri = places[:, None] >= places[None, :]

    def block_step(state, item):
        x_blk, b_blk, c_blk, step_blk, rate_blk, reset_blk = item
        running = jnp.cumsum(rate_blk, axis=2)
        segment = jnp.cumsum(reset_blk)
        joined = (segment[:, None] == segment[None, :]) & lower_tri
        spread = running[..., :, None] - running[..., None, :]
        weights = jnp.where(joined, jnp.exp(jnp.where(joined, spread, 0.0)), 0.0)
        scores = jnp.einsum('ign,jgn->gij', c_blk, b_blk, precision=exact_prec)
        mixing = weights * scores[:, None] * step_blk[:, :, None, :]
        inside = jnp.einsum('ghij,jghp->ighp', mixing, x_blk, precision=exact_prec)
        opening = segment == 0
        entry_decay = jnp.where(opening, jnp.exp(jnp.where(opening, running, 0.0)), 0.0)
        carried = jnp.einsum('ghi,ign,ghpn->ighp', entry_decay, c_blk, state, precision=exact_prec)
        closing = segment == segment[-1]
        final_sum = running[..., -1:]
        end_weight = jnp.where(closing, jnp.exp(jnp.where(closing, final_sum - running, 0.0)), 0.0) * step_blk
        fresh_state = jnp.einsum('ghj,jghp,jgn->ghpn', end_weight, x_blk, b_blk, precision=exact_prec)
        keeping = jnp.exp(final_sum[..., 0]) * (segment[-1] == 0).astype(jnp.float32)
        return (keeping[..., None, None] * state + fresh_state, inside + carried)
    initial = jnp.zeros((groups, per_group, HEAD_DIM, STATE), jnp.float32)
    _, results = lax.scan(jax.checkpoint(block_step), initial, (x_blocks, b_blocks, c_blocks, step_blocks, rate_blocks, reset_blocks))
    ssd_out = results.reshape(tokens, groups, per_group, HEAD_DIM)
    ssd_out = ssd_out + skip_weight.reshape(groups, per_group)[None, :, :, None] * x_groups
    gated = ssd_out.reshape(tokens, groups, per_group * HEAD_DIM) * jax.nn.silu(gate_f.reshape(tokens, groups, per_group * HEAD_DIM))
    factor = lax.rsqrt(lax.optimization_barrier(jnp.mean(gated * gated, axis=2, keepdims=True)) + norm_epsilon)
    return (gated * factor).reshape(tokens, groups * per_group * HEAD_DIM) * norm_gain[None, :]

def reference(x_in, gate_in, b_in, c_in, dt_raw, dt_bias, a_log, skip_weight, norm_gain, w_out, doc_starts, grad_out):
    places = jnp.arange(TOKENS, dtype=jnp.int32)
    resets = lax.optimization_barrier(jnp.sum((places[:, None] == doc_starts[None, :]).astype(jnp.int32), axis=1))

    def forward(x_f, gate_f, b_f, c_f, dt_f):
        return ssd_forward(x_f, gate_f, b_f, c_f, dt_f, dt_bias, a_log, skip_weight, norm_gain, resets)
    normed, pullback = jax.vjp(forward, x_in.astype(jnp.float32), gate_in.astype(jnp.float32), b_in.astype(jnp.float32), c_in.astype(jnp.float32), dt_raw)
    mixed_out = jnp.dot(normed.astype(jnp.bfloat16), w_out, preferred_element_type=jnp.float32).astype(jnp.bfloat16)
    grad_normed = jnp.dot(grad_out, w_out.T, preferred_element_type=jnp.float32)
    grad_x, grad_gate, grad_b, grad_c, grad_dt = pullback(grad_normed)
    return (mixed_out, grad_x.astype(jnp.bfloat16), grad_gate.astype(jnp.bfloat16), grad_b.astype(jnp.bfloat16), grad_c.astype(jnp.bfloat16), grad_dt)
```

```python
import jax
import jax.numpy as jnp
from jax import lax
from jax.experimental import pallas as pl
from jax.experimental.pallas import tpu as pltpu
from jax.sharding import PartitionSpec as P

F32 = jnp.float32
BF16 = jnp.bfloat16
HIGH = lax.Precision.HIGHEST
RANKS = 16
SHARDS = 16
RING = 8
HEADS = 8
WIDTH = 64
CHANNELS = HEADS * WIDTH
STATE = 256
ROWS = 256
MODEL = 8192
HALF = MODEL // 2
CHIP_ROWS = ROWS // RING
OWN_ROWS = CHIP_ROWS // 2
PIECE = HALF // 2
CHUNK = CHANNELS // RANKS
GROUP_CHANNELS = 2048
EPS = 1e-05


def nn(a, b, precision=None):
    return lax.dot_general(
        a, b, (((1,), (0,)), ((), ())), preferred_element_type=F32, precision=precision
    )


def nt(a, b):
    return lax.dot_general(a, b, (((1,), (1,)), ((), ())), preferred_element_type=F32)


def tn(a, b):
    return lax.dot_general(a, b, (((0,), (0,)), ((), ())), preferred_element_type=F32)


def streams(way, hop):
    if way == 0:
        return (0, 1) if hop else (0,)
    return (1, 0) if hop else (1,)


def layer(
    x_ref,
    gate_ref,
    b_hbm,
    c_hbm,
    dt_ref,
    bias_ref,
    alog_ref,
    skip_ref,
    gain_ref,
    w_hbm,
    docs_ref,
    go_hbm,
    mixed_ref,
    gx_ref,
    gg_ref,
    gbc_ref,
    gdt_ref,
    bv,
    cv,
    wv,
    gbuf,
    xt,
    r_s,
    e_s,
    wend_s,
    step_s,
    qcol,
    mask,
    gt,
    ws,
    mt,
    yin,
    car,
    yt,
    gated,
    sl,
    dsl,
    gcol,
    wxt,
    wxn,
    fsum,
    keep,
    sb,
    rb,
    eb,
    s0,
    sb2,
    rb2,
    eb2,
    zz,
    gn,
    nbuf,
    abuf,
    fc,
    pp,
    rsend,
    rrecv,
    qsend,
    qrecv,
    dyb,
    edy,
    dgt,
    dxin,
    rowdot,
    coldot,
    cardot,
    zdot,
    gown,
    gsend,
    grecv,
    ob,
    orecv,
    loc,
    pair_s,
    pair_r,
    ag_s,
    ag_r,
    rs_s,
    rs_r,
    ex_s,
    ex_r,
    gr_s,
    gr_r,
):
    rank = lax.axis_index("context")
    shard = lax.axis_index("tensor")
    chip = shard // 2
    core = shard % 2
    other = 1 - core
    group = shard // 4
    member = shard % 4
    sibling = chip * 2 + other
    ahead = ((chip + 1) % RING) * 2 + core
    behind = ((chip + RING - 1) % RING) * 2 + core
    mates = (None, 1 + member - 2 * (member % 2), (member + 2) % 4, 3 - member)

    def remote(src, dst, send, recv, c_to, t_to):
        return pltpu.make_async_remote_copy(
            src_ref=src,
            dst_ref=dst,
            send_sem=send,
            recv_sem=recv,
            device_id=(c_to, t_to),
            device_id_type=pl.DeviceIdType.MESH,
        )

    def each(first, last, body):
        def step(i, carry):
            body(i)
            return carry

        lax.fori_loop(first, last, step, 0)

    barrier = pltpu.get_barrier_semaphore()

    def greet(c_to, t_to):
        pl.semaphore_signal(
            barrier, inc=1, device_id=(c_to, t_to), device_id_type=pl.DeviceIdType.MESH
        )

    greet(rank, sibling)
    greet(rank, group * 4 + mates[3])
    greet(rank, ahead)
    greet(rank, behind)
    each(1, RANKS, lambda k: greet((rank + k) % RANKS, shard))

    here = pl.ds(pl.multiple_of(core * HALF, HALF), HALF)
    there = pl.ds(pl.multiple_of(other * HALF, HALF), HALF)
    mine = pl.ds(pl.multiple_of(core * OWN_ROWS, OWN_ROWS), OWN_ROWS)
    columns = pl.ds(pl.multiple_of(group * STATE, STATE), STATE)
    load_go = pltpu.make_async_copy(go_hbm.at[:, here], gbuf.at[chip, mine, :], loc.at[0])
    load_b = pltpu.make_async_copy(b_hbm.at[:, columns], bv, loc.at[1])
    load_c = pltpu.make_async_copy(c_hbm.at[:, columns], cv, loc.at[2])
    load_w = pltpu.make_async_copy(w_hbm.at[:, here], wv.at[core], loc.at[3])
    load_go.start()
    load_b.start()
    load_c.start()
    load_w.start()

    head_rows = lax.broadcasted_iota(jnp.int32, (HEADS, ROWS), 0)

    def per_head(ref):
        total = jnp.zeros((HEADS, ROWS), F32)
        for h in range(HEADS):
            total = jnp.where(head_rows == h, ref[h], total)
        return total

    raw = dt_ref[...] + per_head(bias_ref)
    a_rate = -jnp.exp(per_head(alog_ref))
    step = jnp.maximum(raw, 0.0) + jnp.log1p(jnp.exp(-jnp.abs(raw)))
    row_ids = lax.broadcasted_iota(jnp.int32, (ROWS, ROWS), 0)
    col_ids = lax.broadcasted_iota(jnp.int32, (ROWS, ROWS), 1)
    upto = jnp.where(row_ids <= col_ids, 1.0, 0.0)
    running = nn(step * a_rate, upto, HIGH)
    final = running[:, ROWS - 1 : ROWS]
    base = rank * ROWS
    starts = []
    for i in range(4):
        begin = docs_ref[i]
        starts.append(jnp.where(begin >= base, begin - base, 1 << 20))
    pos_row = lax.broadcasted_iota(jnp.int32, (1, ROWS), 1)
    pos_col = lax.broadcasted_iota(jnp.int32, (ROWS, 1), 0)
    seg_row = jnp.zeros((1, ROWS), jnp.int32)
    seg_col = jnp.zeros((ROWS, 1), jnp.int32)
    seg_last = jnp.int32(0)
    for begin in starts:
        seg_row = seg_row + jnp.where(pos_row >= begin, 1, 0)
        seg_col = seg_col + jnp.where(pos_col >= begin, 1, 0)
        seg_last = seg_last + jnp.where(begin <= ROWS - 1, 1, 0)
    opening = seg_row == 0
    closing = seg_row == seg_last
    r_s[...] = running
    step_s[...] = step
    e_s[...] = jnp.where(opening, jnp.exp(running), 0.0)
    wend_s[...] = jnp.where(closing, jnp.exp(final - running), 0.0) * step
    mask[...] = jnp.where((seg_col == seg_row) & (row_ids <= col_ids), 0.0, -1e30)
    shifted = (running - jnp.log(step)).T
    for h in range(HEADS):
        qcol[h] = jnp.broadcast_to(shifted[:, h : h + 1], (ROWS, 128))
    fsum[rank] = jnp.broadcast_to(final, (HEADS, 128))
    xt[...] = x_ref[...].T.reshape(HEADS, WIDTH, ROWS)

    pl.semaphore_wait(barrier, 4 + RANKS - 1)
    pair_go = remote(
        go_hbm.at[:, there], gbuf.at[chip, mine, :], pair_s.at[0], pair_r.at[0], rank, sibling
    )
    pair_w = remote(w_hbm.at[:, there], wv.at[core], pair_s.at[1], pair_r.at[1], rank, sibling)
    pair_go.start()
    pair_w.start()

    def spread(which, src, dst, own_src):
        def copy(k):
            to = (rank + k) % RANKS
            return remote(
                src.at[rank] if own_src else src.at[to],
                dst.at[rank],
                ex_s.at[which, k],
                ex_r.at[which, k],
                to,
                shard,
            )

        return copy

    ex_keep = spread(0, fsum, fsum, True)
    ex_state = spread(1, sb, rb, False)
    ex_enter = spread(2, eb, s0, False)
    ex_grad = spread(3, sb2, rb2, False)
    ex_later = spread(4, eb2, zz, False)
    each(1, RANKS, lambda k: ex_keep(k).start())

    def ag_copy(hop, way, piece):
        block = (chip + RING - hop) % RING if way == 0 else (chip + hop) % RING
        cols = pl.ds(piece * PIECE, PIECE)
        slot = (hop * 2 + way) * 2 + piece
        return remote(
            gbuf.at[block, :, cols],
            gbuf.at[block, :, cols],
            ag_s.at[slot],
            ag_r.at[slot],
            rank,
            ahead if way == 0 else behind,
        )

    def ag_streams(way, hop):
        return streams(way, 3 - hop)

    def ag_hop(hop):
        for way in range(2):
            for piece in ag_streams(way, hop):
                if hop:
                    ag_copy(hop - 1, way, piece).wait_recv()
                ag_copy(hop, way, piece).start()

    load_go.wait()
    pair_go.wait_recv()
    ag_hop(0)

    load_b.wait()
    load_c.wait()
    for h in range(HEADS):
        wxt[h] = wend_s[h : h + 1, :] * xt[h].astype(F32)
    wx_all = wxt[...].reshape(CHANNELS, ROWS)
    wx_hi = wx_all.astype(BF16)
    wx_lo = (wx_all - wx_hi.astype(F32)).astype(BF16)
    end_state = nn(wx_hi, bv[...]) + nn(wx_lo, bv[...])
    sb[...] = end_state.astype(BF16).reshape(RANKS, CHUNK, STATE)
    each(1, RANKS, lambda k: ex_state(k).start())
    rb[rank] = sb[rank]
    wxn[...] = wx_hi.T

    gt[...] = nt(bv[...], cv[...])

    def inside(h):
        q = qcol[h]
        weight = jnp.exp(r_s[pl.ds(h, 1), :] - jnp.concatenate([q, q], axis=1) + mask[...])
        ws[h] = weight
        mixing = (weight * gt[...]).astype(BF16)
        mt[h] = mixing
        yin[h] = nn(xt[h], mixing)

    each(0, HEADS, inside)
    ag_hop(1)

    each(1, RANKS, lambda k: ex_keep(k).wait_recv())
    for r in range(RANKS):
        count = jnp.int32(0)
        for i in range(4):
            begin = docs_ref[i]
            count = count + jnp.where((begin >= r * ROWS) & (begin < (r + 1) * ROWS), 1, 0)
        whole = jnp.where(count == 0, 1.0, 0.0)
        keep[r] = jnp.exp(fsum[r]) * whole
    my_head = rank // 2

    def keep_of(r):
        row = keep[r, pl.ds(my_head, 1), :]
        return jnp.concatenate([row, row], axis=1)

    each(1, RANKS, lambda k: ex_state(k).wait_recv())
    total = jnp.zeros((CHUNK, STATE), F32)
    for r in range(RANKS):
        eb[r] = total.astype(BF16)
        total = keep_of(r) * total + rb[r].astype(F32)
    each(1, RANKS, lambda k: ex_enter(k).start())
    s0[rank] = eb[rank]

    v = gate_ref[...].T.astype(F32)
    sig = 1.0 / (1.0 + jnp.exp(-v))
    sl[...] = (v * sig).reshape(HEADS, WIDTH, ROWS)
    dsl[...] = (sig * (1.0 + v * (1.0 - sig))).reshape(HEADS, WIDTH, ROWS)
    eye = row_ids == col_ids
    for q in range(CHANNELS // 128):
        line = gain_ref[:, q * 128 : (q + 1) * 128]
        picked = jnp.where(eye[:128, :128], line, 0.0)
        column = jnp.sum(picked, axis=1, keepdims=True)
        gcol[2 * q : 2 * q + 2] = jnp.broadcast_to(column, (128, 128)).reshape(2, WIDTH, 128)
    ag_hop(2)

    each(1, RANKS, lambda k: ex_enter(k).wait_recv())
    enter_all = s0[...].reshape(CHANNELS, STATE)
    car[...] = nt(enter_all, cv[...]).reshape(HEADS, WIDTH, ROWS)

    def finish(h, squares):
        moved = e_s[pl.ds(h, 1), :] * car[h]
        car[h] = moved
        out = yin[h] + moved + skip_ref[h] * xt[h].astype(F32)
        yt[h] = out
        value = out * sl[h]
        gated[h] = value
        return squares + jnp.sum(value * value, axis=0, keepdims=True)

    squares = lax.fori_loop(0, HEADS, finish, jnp.zeros((1, ROWS), F32))
    nbuf[0] = squares

    def mate_copy(which, buf, x):
        return remote(
            buf.at[0],
            buf.at[x],
            gr_s.at[which, x],
            gr_r.at[which, x],
            rank,
            group * 4 + mates[x],
        )

    for x in (1, 2, 3):
        mate_copy(0, nbuf, x).start()
    gain_full = jnp.concatenate([gcol[...], gcol[...]], axis=2)
    scaled = (gated[...] * gain_full).reshape(CHANNELS, ROWS).astype(BF16)
    gn[core] = scaled.T
    pair_gn = remote(gn.at[core], gn.at[core], pair_s.at[2], pair_r.at[2], rank, sibling)
    pair_gn.start()
    ag_hop(3)

    load_w.wait()
    pair_w.wait_recv()
    pair_gn.wait_recv()
    tile = 512

    def product(n):
        cols = pl.ds(pl.multiple_of(n * tile, tile), tile)
        value = nn(gn[0], wv[0, :, cols]) + nn(gn[1], wv[1, :, cols])
        pp[:, :, cols] = value.reshape(RING, CHIP_ROWS, tile)

    each(0, HALF // tile, product)
    for x in (1, 2, 3):
        mate_copy(0, nbuf, x).wait_recv()
    mean = (nbuf[0] + nbuf[1] + nbuf[2] + nbuf[3]) * (1.0 / GROUP_CHANNELS)
    factor = lax.rsqrt(mean + EPS)
    factor_col = jnp.sum(jnp.where(eye, factor, 0.0), axis=1, keepdims=True)
    fc[...] = jnp.broadcast_to(factor_col, (ROWS, 128)).reshape(RING, CHIP_ROWS, 128)

    def own_part(block, piece):
        lanes = fc[block]
        return pp[block, :, piece * PIECE : (piece + 1) * PIECE] * jnp.concatenate(
            [lanes] * (PIECE // 128), axis=1
        )

    def rs_copy(hop, way, piece):
        cols = pl.ds(piece * PIECE, PIECE)
        slot = (hop * 2 + way) * 2 + piece
        return remote(
            rsend.at[way, hop, :, cols],
            rrecv.at[way, hop, :, cols],
            rs_s.at[slot],
            rs_r.at[slot],
            rank,
            ahead if way == 0 else behind,
        )

    def rs_hop(hop):
        for way in range(2):
            block = (chip + 4 - hop) % RING if way == 0 else (chip + 4 + hop) % RING
            for piece in streams(way, hop):
                cols = pl.ds(piece * PIECE, PIECE)
                value = own_part(block, piece)
                if hop and piece in streams(way, hop - 1):
                    rs_copy(hop - 1, way, piece).wait_recv()
                    value = value + rrecv[way, hop - 1, :, cols].astype(F32)
                rsend[way, hop, :, cols] = value.astype(BF16)
                rs_copy(hop, way, piece).start()

    rs_hop(0)

    for way in range(2):
        for piece in range(2):
            hop = 3 if piece in ag_streams(way, 3) else 2
            ag_copy(hop, way, piece).wait_recv()
    cotangent = gbuf[...].reshape(ROWS, HALF)
    qsend[...] = nt(wv[other], cotangent)
    pair_q = remote(qsend, qrecv, pair_s.at[3], pair_r.at[3], rank, sibling)
    pair_q.start()
    grad_own = nt(wv[core], cotangent)
    rs_hop(1)
    pair_q.wait_recv()
    grad_scaled = (grad_own + qrecv[...]).reshape(HEADS, WIDTH, ROWS) * gain_full
    along = jnp.sum(
        (grad_scaled * gated[...]).reshape(CHANNELS, ROWS), axis=0, keepdims=True
    )
    abuf[0] = along
    for x in (1, 2, 3):
        mate_copy(1, abuf, x).start()
    for x in (1, 2, 3):
        mate_copy(1, abuf, x).wait_recv()
    along = abuf[0] + abuf[1] + abuf[2] + abuf[3]
    bend = factor * factor * factor * along * (1.0 / GROUP_CHANNELS)
    grad_gated = grad_scaled * factor[None] - gated[...] * bend[None]
    dy_all = grad_gated * sl[...]
    dyb[...] = dy_all.astype(BF16)
    grad_gate = (grad_gated * yt[...] * dsl[...]).astype(BF16)
    gg_ref[...] = grad_gate.reshape(CHANNELS, ROWS).T

    for h in range(HEADS):
        edy[h] = (e_s[h : h + 1, :] * dyb[h].astype(F32)).astype(BF16)
    edy_all = edy[...].reshape(CHANNELS, ROWS)
    sb2[...] = nn(edy_all, cv[...]).astype(BF16).reshape(RANKS, CHUNK, STATE)
    each(1, RANKS, lambda k: ex_grad(k).start())
    rb2[rank] = sb2[rank]

    dgt[...] = jnp.zeros((ROWS, ROWS), F32)

    def back(h):
        dy = dyb[h]
        x_now = xt[h]
        dgt[...] += ws[h] * tn(x_now, dy)
        grad_in = nt(dy, mt[h])
        dxin[h] = grad_in
        dyf = dy.astype(F32)
        rowdot[pl.ds(h, 1), :] = jnp.sum(dyf * yin[h], axis=0, keepdims=True)
        cardot[pl.ds(h, 1), :] = jnp.sum(dyf * car[h], axis=0, keepdims=True)
        coldot[pl.ds(h, 1), :] = jnp.sum(x_now.astype(F32) * grad_in, axis=0, keepdims=True)

    each(0, HEADS, back)
    rs_hop(2)

    each(1, RANKS, lambda k: ex_grad(k).wait_recv())
    total = jnp.zeros((CHUNK, STATE), F32)
    for r in reversed(range(RANKS)):
        eb2[r] = total.astype(BF16)
        total = keep_of(r) * total + rb2[r].astype(F32)
    each(1, RANKS, lambda k: ex_later(k).start())
    zz[rank] = eb2[rank]

    grad_scores = dgt[...].astype(BF16)
    grad_c = tn(grad_scores, bv[...]) + nn(edy_all.T, enter_all)
    grad_b = nn(grad_scores, cv[...])
    rs_hop(3)

    each(1, RANKS, lambda k: ex_later(k).wait_recv())
    later = zz[...].reshape(CHANNELS, STATE)
    grad_b = grad_b + nn(wxn[...], later)
    lane = lax.broadcasted_iota(jnp.int32, (ROWS, 128), 1)
    for q in range(2):
        tile_b = grad_b[:, q * 128 : (q + 1) * 128]
        tile_c = grad_c[:, q * 128 : (q + 1) * 128]
        gown[2 * q] = jnp.where(lane < 64, tile_b, pltpu.roll(tile_c, 64, 1))
        gown[2 * q + 1] = jnp.where(lane < 64, pltpu.roll(tile_b, 64, 1), tile_c)
    gsend[...] = gown[...].astype(BF16)

    def share_copy(x):
        return remote(
            gsend.at[mates[x]],
            grecv.at[x],
            gr_s.at[2, x],
            gr_r.at[2, x],
            rank,
            group * 4 + mates[x],
        )

    for x in (1, 2, 3):
        share_copy(x).start()

    moved_back = nt(later, bv[...])
    inner = jnp.zeros((HEADS, ROWS), F32)
    overlap = later.astype(F32) * enter_all.astype(F32)
    for h in range(HEADS):
        part = moved_back[h * WIDTH : (h + 1) * WIDTH, :]
        part = wend_s[h : h + 1, :] * part
        x_now = xt[h].astype(F32)
        zdot[h : h + 1, :] = jnp.sum(x_now * part, axis=0, keepdims=True)
        dxin[h] = dxin[h] + part + skip_ref[h] * dyb[h].astype(F32)
        block = overlap[h * WIDTH : (h + 1) * WIDTH, :]
        inner = jnp.where(head_rows == h, jnp.sum(block), inner)
    gx_ref[...] = dxin[...].reshape(CHANNELS, ROWS).astype(BF16).T

    from_here = jnp.where(row_ids >= col_ids, 1.0, 0.0)
    before = jnp.where(row_ids < col_ids, 1.0, 0.0)
    kept = jnp.where(seg_last == 0, 1.0, 0.0) * jnp.exp(final)
    grad_rate = (
        nn(rowdot[...] - coldot[...] + cardot[...], from_here, HIGH)
        + nn(zdot[...], before, HIGH)
        + kept * inner
    )
    grad_step = (coldot[...] + zdot[...]) / step_s[...] + a_rate * grad_rate
    gdt_ref[...] = grad_step * (1.0 / (1.0 + jnp.exp(-raw)))

    for way in range(2):
        for piece in range(2):
            rs_copy(3, way, piece).wait_recv()
    for piece in range(2):
        cols = pl.ds(piece * PIECE, PIECE)
        value = (
            own_part(chip, piece)
            + rrecv[0, 3, :, cols].astype(F32)
            + rrecv[1, 3, :, cols].astype(F32)
        )
        ob[:, :, cols] = value.astype(BF16).reshape(2, OWN_ROWS, PIECE)
    pair_out = remote(ob.at[other], orecv, pair_s.at[4], pair_r.at[4], rank, sibling)
    pair_out.start()
    mixed_ref[:, here] = ob[core]
    for x in (1, 2, 3):
        share_copy(x).wait_recv()
    shares = gown[member]
    for x in (1, 2, 3):
        shares = shares + grecv[x].astype(F32)
    gbc_ref[...] = shares.astype(BF16)
    pair_out.wait_recv()
    mixed_ref[:, there] = orecv[...]

    for copy in (pair_go, pair_w, pair_gn, pair_q, pair_out):
        copy.wait_send()
    for hop in range(4):
        for way in range(2):
            for piece in ag_streams(way, hop):
                ag_copy(hop, way, piece).wait_send()
            for piece in streams(way, hop):
                rs_copy(hop, way, piece).wait_send()
    for exchange in (ex_keep, ex_state, ex_enter, ex_grad, ex_later):
        each(1, RANKS, lambda k: exchange(k).wait_send())
    for x in (1, 2, 3):
        mate_copy(0, nbuf, x).wait_send()
        mate_copy(1, abuf, x).wait_send()
        share_copy(x).wait_send()


def on_device(
    x_in,
    gate_in,
    b_in,
    c_in,
    dt_raw,
    dt_bias,
    a_log,
    skip_weight,
    norm_gain,
    w_out,
    doc_starts,
    grad_out,
):
    vmem = pl.BlockSpec(memory_space=pltpu.VMEM)
    smem = pl.BlockSpec(memory_space=pltpu.SMEM)
    anywhere = pl.BlockSpec(memory_space=pl.ANY)
    by_head = (HEADS, WIDTH, ROWS)
    by_rank = (RANKS, CHUNK, STATE)
    dma = pltpu.SemaphoreType.DMA
    out = pl.pallas_call(
        layer,
        out_shape=[
            jax.ShapeDtypeStruct((OWN_ROWS, MODEL), BF16),
            jax.ShapeDtypeStruct((ROWS, CHANNELS), BF16),
            jax.ShapeDtypeStruct((ROWS, CHANNELS), BF16),
            jax.ShapeDtypeStruct((ROWS, 128), BF16),
            jax.ShapeDtypeStruct((HEADS, ROWS), F32),
        ],
        in_specs=[
            vmem,
            vmem,
            anywhere,
            anywhere,
            vmem,
            smem,
            smem,
            smem,
            vmem,
            anywhere,
            smem,
            anywhere,
        ],
        out_specs=[vmem] * 5,
        scratch_shapes=[
            pltpu.VMEM((ROWS, STATE), BF16),
            pltpu.VMEM((ROWS, STATE), BF16),
            pltpu.VMEM((2, CHANNELS, HALF), BF16),
            pltpu.VMEM((RING, CHIP_ROWS, HALF), BF16),
            pltpu.VMEM(by_head, BF16),
            pltpu.VMEM((HEADS, ROWS), F32),
            pltpu.VMEM((HEADS, ROWS), F32),
            pltpu.VMEM((HEADS, ROWS), F32),
            pltpu.VMEM((HEADS, ROWS), F32),
            pltpu.VMEM((HEADS, ROWS, 128), F32),
            pltpu.VMEM((ROWS, ROWS), F32),
            pltpu.VMEM((ROWS, ROWS), F32),
            pltpu.VMEM((HEADS, ROWS, ROWS), F32),
            pltpu.VMEM((HEADS, ROWS, ROWS), BF16),
            pltpu.VMEM(by_head, F32),
            pltpu.VMEM(by_head, F32),
            pltpu.VMEM(by_head, F32),
            pltpu.VMEM(by_head, F32),
            pltpu.VMEM(by_head, F32),
            pltpu.VMEM(by_head, F32),
            pltpu.VMEM((HEADS, WIDTH, 128), F32),
            pltpu.VMEM(by_head, F32),
            pltpu.VMEM((ROWS, CHANNELS), BF16),
            pltpu.VMEM((RANKS, HEADS, 128), F32),
            pltpu.VMEM((RANKS, HEADS, 128), F32),
            pltpu.VMEM(by_rank, BF16),
            pltpu.VMEM(by_rank, BF16),
            pltpu.VMEM(by_rank, BF16),
            pltpu.VMEM(by_rank, BF16),
            pltpu.VMEM(by_rank, BF16),
            pltpu.VMEM(by_rank, BF16),
            pltpu.VMEM(by_rank, BF16),
            pltpu.VMEM(by_rank, BF16),
            pltpu.VMEM((2, ROWS, CHANNELS), BF16),
            pltpu.VMEM((4, 1, ROWS), F32),
            pltpu.VMEM((4, 1, ROWS), F32),
            pltpu.VMEM((RING, CHIP_ROWS, 128), F32),
            pltpu.VMEM((RING, CHIP_ROWS, HALF), F32),
            pltpu.VMEM((2, 4, CHIP_ROWS, HALF), BF16),
            pltpu.VMEM((2, 4, CHIP_ROWS, HALF), BF16),
            pltpu.VMEM((CHANNELS, ROWS), F32),
            pltpu.VMEM((CHANNELS, ROWS), F32),
            pltpu.VMEM(by_head, BF16),
            pltpu.VMEM(by_head, BF16),
            pltpu.VMEM((ROWS, ROWS), F32),
            pltpu.VMEM(by_head, F32),
            pltpu.VMEM((HEADS, ROWS), F32),
            pltpu.VMEM((HEADS, ROWS), F32),
            pltpu.VMEM((HEADS, ROWS), F32),
            pltpu.VMEM((HEADS, ROWS), F32),
            pltpu.VMEM((4, ROWS, 128), F32),
            pltpu.VMEM((4, ROWS, 128), BF16),
            pltpu.VMEM((4, ROWS, 128), BF16),
            pltpu.VMEM((2, OWN_ROWS, HALF), BF16),
            pltpu.VMEM((OWN_ROWS, HALF), BF16),
            dma((4,)),
            dma((5,)),
            dma((5,)),
            dma((16,)),
            dma((16,)),
            dma((16,)),
            dma((16,)),
            dma((5, RANKS)),
            dma((5, RANKS)),
            dma((3, 4)),
            dma((3, 4)),
        ],
        compiler_params=pltpu.CompilerParams(
            collective_id=0, has_side_effects=True, vmem_limit_bytes=56 * 1024 * 1024
        ),
        cost_estimate=pl.CostEstimate(
            flops=6_000_000_000, bytes_accessed=16_000_000, transcendentals=1_000_000
        ),
        name="layer",
    )(
        x_in,
        gate_in,
        b_in,
        c_in,
        dt_raw,
        dt_bias,
        a_log,
        skip_weight,
        norm_gain.reshape(1, CHANNELS),
        w_out,
        doc_starts,
        grad_out,
    )
    mixed, grad_x, grad_gate, grad_bc, grad_dt = out
    return (mixed, grad_x, grad_gate, grad_bc[:, :64], grad_bc[:, 64:], grad_dt)


def solution(mesh):
    return jax.shard_map(
        on_device,
        mesh=mesh,
        in_specs=(
            P("context", "tensor"),
            P("context", "tensor"),
            P("context", None),
            P("context", None),
            P("tensor", "context"),
            P("tensor"),
            P("tensor"),
            P("tensor"),
            P("tensor"),
            P("tensor", None),
            P(),
            P(("context", "tensor"), None),
        ),
        out_specs=(
            P(("context", "tensor"), None),
            P("context", "tensor"),
            P("context", "tensor"),
            P("context", "tensor"),
            P("context", "tensor"),
            P("tensor", "context"),
        ),
        check_vma=False,
    )
```

```python
import jax
import jax.numpy as jnp
from jax import lax
from jax.experimental import pallas as pl
from jax.experimental.pallas import tpu as pltpu
from jax.sharding import PartitionSpec as P

F32 = jnp.float32
BF16 = jnp.bfloat16
HIGH = lax.Precision.HIGHEST
RANKS = 16
SHARDS = 16
RING = 8
HEADS = 8
WIDTH = 64
CHANNELS = HEADS * WIDTH
STATE = 256
ROWS = 256
MODEL = 8192
HALF = MODEL // 2
CHIP_ROWS = ROWS // RING
OWN_ROWS = CHIP_ROWS // 2
PIECE = HALF // 2
CHUNK = CHANNELS // RANKS
GROUP_CHANNELS = 2048
EPS = 1e-05


def nn(a, b, precision=None):
    return lax.dot_general(
        a, b, (((1,), (0,)), ((), ())), preferred_element_type=F32, precision=precision
    )


def nt(a, b):
    return lax.dot_general(a, b, (((1,), (1,)), ((), ())), preferred_element_type=F32)


def tn(a, b):
    return lax.dot_general(a, b, (((0,), (0,)), ((), ())), preferred_element_type=F32)


def layer(
    x_hbm,
    gate_hbm,
    b_hbm,
    c_hbm,
    dt_hbm,
    bias_ref,
    alog_ref,
    skip_ref,
    gain_hbm,
    w_hbm,
    docs_ref,
    go_hbm,
    mixed_out,
    gx_out,
    gg_out,
    gb_out,
    gc_out,
    gdt_out,
    x_ref,
    gate_ref,
    dt_ref,
    gain_ref,
    gx_ref,
    gg_ref,
    gb_ref,
    gc_ref,
    gdt_ref,
    bv,
    cv,
    wv,
    gbuf,
    xt,
    r_s,
    e_s,
    wend_s,
    step_s,
    qcol,
    mask,
    gt,
    ws,
    mt,
    yin,
    car,
    yt,
    gated,
    sl,
    dsl,
    gcol,
    wxh,
    cvt,
    fsum,
    keep,
    sb,
    rb,
    eb,
    s0,
    sb2,
    rb2,
    eb2,
    zz,
    gn,
    nbuf,
    abuf,
    fc,
    pp,
    rsend,
    rrecv,
    qsend,
    qrecv,
    dyb,
    edy,
    dgt,
    dxin,
    rowdot,
    coldot,
    cardot,
    zdot,
    gown,
    gsend,
    grecv,
    ob,
    orecv,
    loc,
    out_s,
    pair_s,
    pair_r,
    ag_s,
    ag_r,
    rs_s,
    rs_r,
    ex_s,
    ex_r,
    gr_s,
    gr_r,
):
    rank = lax.axis_index("context")
    shard = lax.axis_index("tensor")
    chip = shard // 2
    core = shard % 2
    other = 1 - core
    group = shard // 4
    member = shard % 4
    sibling = chip * 2 + other
    ahead = ((chip + 1) % RING) * 2 + core
    behind = ((chip + RING - 1) % RING) * 2 + core
    mates = (None, 1 + member - 2 * (member % 2), (member + 2) % 4, 3 - member)

    def remote(src, dst, send, recv, c_to, t_to):
        return pltpu.make_async_remote_copy(
            src_ref=src,
            dst_ref=dst,
            send_sem=send,
            recv_sem=recv,
            device_id=(c_to, t_to),
            device_id_type=pl.DeviceIdType.MESH,
        )

    def each(first, last, body, unroll=1):
        def step(i, carry):
            body(i)
            return carry

        lax.fori_loop(first, last, step, 0, unroll=unroll)

    barrier = pltpu.get_barrier_semaphore()

    def greet(c_to, t_to):
        pl.semaphore_signal(
            barrier, inc=1, device_id=(c_to, t_to), device_id_type=pl.DeviceIdType.MESH
        )

    greet(rank, sibling)
    greet(rank, group * 4 + mates[3])
    greet(rank, ahead)
    greet(rank, behind)
    each(1, RANKS, lambda k: greet((rank + k) % RANKS, shard))

    here = pl.ds(pl.multiple_of(core * HALF, HALF), HALF)
    there = pl.ds(pl.multiple_of(other * HALF, HALF), HALF)
    columns = pl.ds(pl.multiple_of(group * STATE, STATE), STATE)
    load_dt = pltpu.make_async_copy(dt_hbm, dt_ref, loc.at[0])
    load_x = pltpu.make_async_copy(x_hbm, x_ref, loc.at[1])
    load_b = pltpu.make_async_copy(b_hbm.at[:, columns], bv, loc.at[2])
    load_c = pltpu.make_async_copy(c_hbm.at[:, columns], cv, loc.at[3])
    load_gate = pltpu.make_async_copy(gate_hbm, gate_ref, loc.at[4])
    load_gain = pltpu.make_async_copy(gain_hbm, gain_ref, loc.at[5])
    load_go = pltpu.make_async_copy(go_hbm.at[:, here], gbuf.at[chip, core], loc.at[6])
    load_w = pltpu.make_async_copy(w_hbm.at[:, here], wv.at[core], loc.at[7])
    for copy in (load_dt, load_x, load_b, load_c, load_gate, load_gain, load_go, load_w):
        copy.start()

    head_rows = lax.broadcasted_iota(jnp.int32, (HEADS, ROWS), 0)

    def per_head(ref):
        total = jnp.zeros((HEADS, ROWS), F32)
        for h in range(HEADS):
            total = jnp.where(head_rows == h, ref[h], total)
        return total

    load_dt.wait()
    raw = dt_ref[...] + per_head(bias_ref)
    a_rate = -jnp.exp(per_head(alog_ref))
    step = jnp.maximum(raw, 0.0) + jnp.log1p(jnp.exp(-jnp.abs(raw)))
    row_ids = lax.broadcasted_iota(jnp.int32, (ROWS, ROWS), 0)
    col_ids = lax.broadcasted_iota(jnp.int32, (ROWS, ROWS), 1)
    upto = jnp.where(row_ids <= col_ids, 1.0, 0.0)
    running = nn(step * a_rate, upto, HIGH)
    final = running[:, ROWS - 1 : ROWS]
    base = rank * ROWS
    starts = []
    for i in range(4):
        begin = docs_ref[i]
        starts.append(jnp.where(begin >= base, begin - base, 1 << 20))
    pos_row = lax.broadcasted_iota(jnp.int32, (1, ROWS), 1)
    pos_col = lax.broadcasted_iota(jnp.int32, (ROWS, 1), 0)
    seg_row = jnp.zeros((1, ROWS), jnp.int32)
    seg_col = jnp.zeros((ROWS, 1), jnp.int32)
    seg_last = jnp.int32(0)
    for begin in starts:
        seg_row = seg_row + jnp.where(pos_row >= begin, 1, 0)
        seg_col = seg_col + jnp.where(pos_col >= begin, 1, 0)
        seg_last = seg_last + jnp.where(begin <= ROWS - 1, 1, 0)
    opening = seg_row == 0
    closing = seg_row == seg_last
    r_s[...] = running
    step_s[...] = step
    e_s[...] = jnp.where(opening, jnp.exp(running), 0.0)
    wend_s[...] = jnp.where(closing, jnp.exp(final - running), 0.0) * step
    fsum[rank] = jnp.broadcast_to(final, (HEADS, 128))

    load_x.wait()
    load_b.wait()
    xt[...] = x_ref[...].T.reshape(HEADS, WIDTH, ROWS)
    for h in range(HEADS):
        wx = wend_s[h : h + 1, :] * xt[h].astype(F32)
        wx_hi = wx.astype(BF16)
        wx_lo = (wx - wx_hi.astype(F32)).astype(BF16)
        wxh[h] = wx_hi
        end_state = nn(wx_hi, bv[...]) + nn(wx_lo, bv[...])
        sb[2 * h : 2 * h + 2] = end_state.astype(BF16).reshape(2, CHUNK, STATE)
    rb[rank] = sb[rank]

    pl.semaphore_wait(barrier, 4 + RANKS - 1)
    pair_go = remote(
        go_hbm.at[:, there], gbuf.at[chip, core], pair_s.at[0], pair_r.at[0], rank, sibling
    )
    pair_w = remote(w_hbm.at[:, there], wv.at[core], pair_s.at[1], pair_r.at[1], rank, sibling)

    def spread(which, src, dst, own_src):
        def copy(k):
            to = (rank + k) % RANKS
            return remote(
                src.at[rank] if own_src else src.at[to],
                dst.at[rank],
                ex_s.at[which, k],
                ex_r.at[which, k],
                to,
                shard,
            )

        return copy

    ex_keep = spread(0, fsum, fsum, True)
    ex_state = spread(1, sb, rb, False)
    ex_enter = spread(2, eb, s0, False)
    ex_grad = spread(3, sb2, rb2, False)
    ex_later = spread(4, eb2, zz, False)

    def ag_copy(hop, way, piece):
        block = (chip + RING - hop) % RING if way == 0 else (chip + hop) % RING
        half = core if piece == 0 else other
        slot = (hop * 2 + way) * 2 + piece
        first = hop == 0 and piece == 0
        return remote(
            go_hbm.at[:, here] if first else gbuf.at[block, half],
            gbuf.at[block, half],
            ag_s.at[slot],
            ag_r.at[slot],
            rank,
            ahead if way == 0 else behind,
        )

    def ag_step(hop, piece):
        for way in range(2):
            if hop < 3 or way == piece:
                if hop:
                    ag_copy(hop - 1, way, piece).wait_recv()
                ag_copy(hop, way, piece).start()

    pair_go.start()
    ag_step(0, 0)
    each(1, RANKS, lambda k: ex_state(k).start())
    each(1, RANKS, lambda k: ex_keep(k).start())
    pair_w.start()
    pair_go.wait_recv()
    ag_step(0, 1)

    mask[...] = jnp.where((seg_col == seg_row) & (row_ids <= col_ids), 0.0, -1e30)
    shifted = (running - jnp.log(step)).T
    for h in range(HEADS):
        qcol[h] = jnp.broadcast_to(shifted[:, h : h + 1], (ROWS, 128))

    load_c.wait()
    gt[...] = nt(bv[...], cv[...])

    def inside(h):
        q = qcol[h]
        weight = jnp.exp(r_s[pl.ds(h, 1), :] - jnp.concatenate([q, q], axis=1) + mask[...])
        ws[h] = weight
        mixing = (weight * gt[...]).astype(BF16)
        mt[h] = mixing
        yin[h] = nn(xt[h], mixing)

    each(0, HEADS, inside, 2)
    ag_step(1, 0)

    each(1, RANKS, lambda k: ex_keep(k).wait_recv())
    for r in range(RANKS):
        count = jnp.int32(0)
        for i in range(4):
            begin = docs_ref[i]
            count = count + jnp.where((begin >= r * ROWS) & (begin < (r + 1) * ROWS), 1, 0)
        whole = jnp.where(count == 0, 1.0, 0.0)
        keep[r] = jnp.exp(fsum[r]) * whole
    my_head = rank // 2

    def keep_of(r):
        row = keep[r, pl.ds(my_head, 1), :]
        return jnp.concatenate([row, row], axis=1)

    each(1, RANKS, lambda k: ex_state(k).wait_recv())
    total = jnp.zeros((CHUNK, STATE), F32)
    for r in range(RANKS):
        eb[r] = total.astype(BF16)
        total = keep_of(r) * total + rb[r].astype(F32)
    each(1, RANKS, lambda k: ex_enter(k).start())
    s0[rank] = eb[rank]
    ag_step(1, 1)

    load_gate.wait()
    load_gain.wait()
    v = gate_ref[...].T.astype(F32)
    sig = 1.0 / (1.0 + jnp.exp(-v))
    sl[...] = (v * sig).reshape(HEADS, WIDTH, ROWS)
    dsl[...] = (sig * (1.0 + v * (1.0 - sig))).reshape(HEADS, WIDTH, ROWS)
    eye = row_ids == col_ids
    for q in range(CHANNELS // 128):
        line = gain_ref[:, q * 128 : (q + 1) * 128]
        picked = jnp.where(eye[:128, :128], line, 0.0)
        column = jnp.sum(picked, axis=1, keepdims=True)
        gcol[2 * q : 2 * q + 2] = jnp.broadcast_to(column, (128, 128)).reshape(2, WIDTH, 128)
    cvt[...] = cv[...].T
    ag_step(2, 0)
    ag_step(2, 1)

    each(1, RANKS, lambda k: ex_enter(k).wait_recv())
    enter_all = s0[...].reshape(CHANNELS, STATE)
    car[...] = nt(enter_all, cv[...]).reshape(HEADS, WIDTH, ROWS)

    def finish(h, squares):
        moved = e_s[pl.ds(h, 1), :] * car[h]
        car[h] = moved
        out = yin[h] + moved + skip_ref[h] * xt[h].astype(F32)
        yt[h] = out
        value = out * sl[h]
        gated[h] = value
        return squares + jnp.sum(value * value, axis=0, keepdims=True)

    squares = lax.fori_loop(0, HEADS, finish, jnp.zeros((1, ROWS), F32))
    nbuf[0] = squares

    def mate_copy(which, buf, x):
        return remote(
            buf.at[0],
            buf.at[x],
            gr_s.at[which, x],
            gr_r.at[which, x],
            rank,
            group * 4 + mates[x],
        )

    for x in (1, 2, 3):
        mate_copy(0, nbuf, x).start()
    gain_full = jnp.concatenate([gcol[...], gcol[...]], axis=2)
    scaled = (gated[...] * gain_full).reshape(CHANNELS, ROWS)
    scaled_hi = scaled.astype(BF16)
    scaled_lo = (scaled - scaled_hi.astype(F32)).astype(BF16)
    gn[core, 0] = scaled_hi.T
    gn[core, 1] = scaled_lo.T
    pair_gn = remote(gn.at[core], gn.at[core], pair_s.at[2], pair_r.at[2], rank, sibling)
    pair_gn.start()
    ag_step(3, 0)

    load_w.wait()
    pair_w.wait_recv()
    pair_gn.wait_recv()
    tile = 512

    def product(n):
        cols = pl.ds(pl.multiple_of(n * tile, tile), tile)
        value = jnp.zeros((ROWS, tile), F32)
        for one in range(2):
            for part in range(2):
                value = value + nn(gn[one, part], wv[one, :, cols])
        pp[:, :, cols] = value.reshape(RING, CHIP_ROWS, tile)

    each(0, HALF // tile // 2, product)
    ag_step(3, 1)
    each(HALF // tile // 2, HALF // tile, product)

    load_go.wait()
    for way in range(2):
        for piece in range(2):
            ag_copy(3 if way == piece else 2, way, piece).wait_recv()

    def fold(n, total):
        cols = pl.ds(pl.multiple_of(n * tile, tile), tile)
        both = gbuf[:, :, :, cols].reshape(ROWS, tile).astype(F32) * pp[:, :, cols].reshape(
            ROWS, tile
        )
        for i in range(tile // 128):
            total = total + both[:, i * 128 : (i + 1) * 128]
        return total

    along_col = jnp.sum(
        lax.fori_loop(0, HALF // tile, fold, jnp.zeros((ROWS, 128), F32)), axis=1, keepdims=True
    )
    abuf[0] = jnp.sum(jnp.where(eye, along_col, 0.0), axis=0, keepdims=True)
    for x in (1, 2, 3):
        mate_copy(1, abuf, x).start()
    for x in (1, 2, 3):
        mate_copy(0, nbuf, x).wait_recv()
    mean = (nbuf[0] + nbuf[1] + nbuf[2] + nbuf[3]) * (1.0 / GROUP_CHANNELS)
    factor = lax.rsqrt(mean + EPS)
    factor_col = jnp.sum(jnp.where(eye, factor, 0.0), axis=1, keepdims=True)
    fc[...] = jnp.broadcast_to(factor_col, (ROWS, 128)).reshape(RING, CHIP_ROWS, 128)

    def own_part(block, piece):
        lanes = fc[block]
        return pp[block, :, piece * PIECE : (piece + 1) * PIECE] * jnp.concatenate(
            [lanes] * (PIECE // 128), axis=1
        )

    def rs_copy(hop, way, piece):
        cols = pl.ds(piece * PIECE, PIECE)
        slot = (hop * 2 + way) * 2 + piece
        return remote(
            rsend.at[way, hop, :, cols],
            rrecv.at[way, hop, :, cols],
            rs_s.at[slot],
            rs_r.at[slot],
            rank,
            ahead if way == 0 else behind,
        )

    def rs_step(hop, turn):
        for way in range(2):
            piece = (way + turn) % 2
            block = (chip + 4 - hop) % RING if way == 0 else (chip + 4 + hop) % RING
            cols = pl.ds(piece * PIECE, PIECE)
            value = own_part(block, piece)
            if hop > turn:
                rs_copy(hop - 1, way, piece).wait_recv()
                value = value + rrecv[way, hop - 1, :, cols].astype(F32)
            rsend[way, hop, :, cols] = value.astype(BF16)
            rs_copy(hop, way, piece).start()

    rs_step(0, 0)

    cotangent = gbuf[...].reshape(ROWS, HALF)
    qsend[...] = nt(wv[other], cotangent)
    pair_q = remote(qsend, qrecv, pair_s.at[3], pair_r.at[3], rank, sibling)
    pair_q.start()
    rs_step(1, 1)
    grad_own = nt(wv[core], cotangent)
    pair_q.wait_recv()
    grad_scaled = (grad_own + qrecv[...]).reshape(HEADS, WIDTH, ROWS) * gain_full
    for x in (1, 2, 3):
        mate_copy(1, abuf, x).wait_recv()
    along = abuf[0] + abuf[1] + abuf[2] + abuf[3]
    bend = factor * factor * factor * along * (1.0 / GROUP_CHANNELS)
    grad_gated = grad_scaled * factor[None] - gated[...] * bend[None]
    dy_all = grad_gated * sl[...]
    dyb[...] = dy_all.astype(BF16)
    grad_gate = (grad_gated * yt[...] * dsl[...]).astype(BF16)
    for h in range(HEADS):
        edy[h] = (e_s[h : h + 1, :] * dyb[h].astype(F32)).astype(BF16)
    edy_all = edy[...].reshape(CHANNELS, ROWS)
    sb2[...] = nn(edy_all, cv[...]).astype(BF16).reshape(RANKS, CHUNK, STATE)
    each(1, RANKS, lambda k: ex_grad(k).start())
    rb2[rank] = sb2[rank]
    rs_step(1, 0)
    gg_ref[...] = grad_gate.reshape(CHANNELS, ROWS).T

    def leave(which, source, target):
        return pltpu.make_async_copy(source, target, out_s.at[which])

    leave_gg = leave(0, gg_ref, gg_out)
    leave_gg.start()

    dgt[...] = jnp.zeros((ROWS, ROWS), F32)

    def back(h):
        dy = dyb[h]
        x_now = xt[h]
        dgt[...] += ws[h] * tn(x_now, dy)
        grad_in = nt(dy, mt[h])
        dxin[h] = grad_in
        dyf = dy.astype(F32)
        rowdot[pl.ds(h, 1), :] = jnp.sum(dyf * yin[h], axis=0, keepdims=True)
        cardot[pl.ds(h, 1), :] = jnp.sum(dyf * car[h], axis=0, keepdims=True)
        coldot[pl.ds(h, 1), :] = jnp.sum(x_now.astype(F32) * grad_in, axis=0, keepdims=True)

    each(0, HEADS, back, 2)
    rs_step(2, 1)
    rs_step(2, 0)

    each(1, RANKS, lambda k: ex_grad(k).wait_recv())
    total = jnp.zeros((CHUNK, STATE), F32)
    for r in reversed(range(RANKS)):
        eb2[r] = total.astype(BF16)
        total = keep_of(r) * total + rb2[r].astype(F32)
    each(1, RANKS, lambda k: ex_later(k).start())
    zz[rank] = eb2[rank]

    def share_copy(which, x):
        return remote(
            gsend.at[which, mates[x]],
            grecv.at[which, x],
            gr_s.at[2 + which, x],
            gr_r.at[2 + which, x],
            rank,
            group * 4 + mates[x],
        )

    grad_scores = dgt[...].astype(BF16)
    grad_c = tn(bv[...], grad_scores) + tn(enter_all, edy_all)
    gown[1] = grad_c.reshape(4, WIDTH, ROWS)
    gsend[1] = gown[1].astype(BF16)
    for x in (1, 2, 3):
        share_copy(1, x).start()
    grad_b = nt(cvt[...], grad_scores)
    from_here = jnp.where(row_ids >= col_ids, 1.0, 0.0)
    before = jnp.where(row_ids < col_ids, 1.0, 0.0)
    kept = jnp.where(seg_last == 0, 1.0, 0.0) * jnp.exp(final)
    grad_rate = nn(rowdot[...] - coldot[...] + cardot[...], from_here, HIGH)

    rs_step(3, 1)
    rs_step(3, 0)

    each(1, RANKS, lambda k: ex_later(k).wait_recv())
    later = zz[...].reshape(CHANNELS, STATE)
    grad_b = grad_b + tn(later, wxh[...].reshape(CHANNELS, ROWS))
    gown[0] = grad_b.reshape(4, WIDTH, ROWS)
    gsend[0] = gown[0].astype(BF16)
    for x in (1, 2, 3):
        share_copy(0, x).start()

    moved_back = nt(later, bv[...])
    inner = jnp.zeros((HEADS, ROWS), F32)
    overlap = later.astype(F32) * enter_all.astype(F32)
    for h in range(HEADS):
        part = moved_back[h * WIDTH : (h + 1) * WIDTH, :]
        part = wend_s[h : h + 1, :] * part
        x_now = xt[h].astype(F32)
        zdot[h : h + 1, :] = jnp.sum(x_now * part, axis=0, keepdims=True)
        dxin[h] = dxin[h] + part + skip_ref[h] * dyb[h].astype(F32)
        block = overlap[h * WIDTH : (h + 1) * WIDTH, :]
        inner = jnp.where(head_rows == h, jnp.sum(block), inner)
    gx_ref[...] = dxin[...].reshape(CHANNELS, ROWS).astype(BF16).T
    leave_gx = leave(2, gx_ref, gx_out)
    leave_gx.start()
    grad_rate = grad_rate + nn(zdot[...], before, HIGH) + kept * inner
    grad_step = (coldot[...] + zdot[...]) / step_s[...] + a_rate * grad_rate
    gdt_ref[...] = grad_step * (1.0 / (1.0 + jnp.exp(-raw)))
    leave_dt = leave(3, gdt_ref, gdt_out)
    leave_dt.start()
    for turn in (1, 0):
        for way in range(2):
            rs_copy(3, way, (way + turn) % 2).wait_recv()
    for piece in range(2):
        cols = pl.ds(piece * PIECE, PIECE)
        value = (
            own_part(chip, piece)
            + rrecv[0, 3, :, cols].astype(F32)
            + rrecv[1, 3, :, cols].astype(F32)
        )
        ob[:, :, cols] = value.astype(BF16).reshape(2, OWN_ROWS, PIECE)
    pair_out = remote(ob.at[other], orecv, pair_s.at[4], pair_r.at[4], rank, sibling)
    pair_out.start()
    leave_mine = leave(1, ob.at[core], mixed_out.at[:, here])
    leave_mine.start()

    pair_out.wait_recv()
    leave_theirs = leave(4, orecv, mixed_out.at[:, there])
    leave_theirs.start()

    def gather(which):
        for x in (1, 2, 3):
            share_copy(which, x).wait_recv()
        shares = gown[which, member]
        for x in (1, 2, 3):
            shares = shares + grecv[which, x].astype(F32)
        return shares.astype(BF16)

    gc_ref[...] = gather(1)
    leave_gc = leave(5, gc_ref, gc_out)
    leave_gc.start()
    gb_ref[...] = gather(0)
    leave_gb = leave(6, gb_ref, gb_out)
    leave_gb.start()

    for copy in (pair_go, pair_w, pair_gn, pair_q, pair_out):
        copy.wait_send()
    for hop in range(4):
        for way in range(2):
            for piece in range(2):
                if hop < 3 or way == piece:
                    ag_copy(hop, way, piece).wait_send()
                if hop or way == piece:
                    rs_copy(hop, way, piece).wait_send()
    for exchange in (ex_keep, ex_state, ex_enter, ex_grad, ex_later):
        each(1, RANKS, lambda k: exchange(k).wait_send())
    for x in (1, 2, 3):
        mate_copy(0, nbuf, x).wait_send()
        mate_copy(1, abuf, x).wait_send()
        share_copy(0, x).wait_send()
        share_copy(1, x).wait_send()
    for copy in (leave_gg, leave_mine, leave_gx, leave_dt, leave_theirs, leave_gc, leave_gb):
        copy.wait()


def hand_out(*refs):
    for source, target in zip(refs[:6], refs[6:]):
        target[...] = source[...]


def on_device(
    x_in,
    gate_in,
    b_in,
    c_in,
    dt_raw,
    dt_bias,
    a_log,
    skip_weight,
    norm_gain,
    w_out,
    doc_starts,
    grad_out,
):
    vmem = pl.BlockSpec(memory_space=pltpu.VMEM)
    smem = pl.BlockSpec(memory_space=pltpu.SMEM)
    anywhere = pl.BlockSpec(memory_space=pl.ANY)
    by_head = (HEADS, WIDTH, ROWS)
    by_rank = (RANKS, CHUNK, STATE)
    dma = pltpu.SemaphoreType.DMA
    out = pl.pallas_call(
        layer,
        out_shape=[
            jax.ShapeDtypeStruct((OWN_ROWS, MODEL), BF16),
            jax.ShapeDtypeStruct((ROWS, CHANNELS), BF16),
            jax.ShapeDtypeStruct((ROWS, CHANNELS), BF16),
            jax.ShapeDtypeStruct((WIDTH, ROWS), BF16),
            jax.ShapeDtypeStruct((WIDTH, ROWS), BF16),
            jax.ShapeDtypeStruct((HEADS, ROWS), F32),
        ],
        in_specs=[
            anywhere,
            anywhere,
            anywhere,
            anywhere,
            anywhere,
            smem,
            smem,
            smem,
            anywhere,
            anywhere,
            smem,
            anywhere,
        ],
        out_specs=[anywhere] * 6,
        scratch_shapes=[
            pltpu.VMEM((ROWS, CHANNELS), BF16),
            pltpu.VMEM((ROWS, CHANNELS), BF16),
            pltpu.VMEM((HEADS, ROWS), F32),
            pltpu.VMEM((1, CHANNELS), F32),
            pltpu.VMEM((ROWS, CHANNELS), BF16),
            pltpu.VMEM((ROWS, CHANNELS), BF16),
            pltpu.VMEM((WIDTH, ROWS), BF16),
            pltpu.VMEM((WIDTH, ROWS), BF16),
            pltpu.VMEM((HEADS, ROWS), F32),
            pltpu.VMEM((ROWS, STATE), BF16),
            pltpu.VMEM((ROWS, STATE), BF16),
            pltpu.VMEM((2, CHANNELS, HALF), BF16),
            pltpu.VMEM((RING, 2, OWN_ROWS, HALF), BF16),
            pltpu.VMEM(by_head, BF16),
            pltpu.VMEM((HEADS, ROWS), F32),
            pltpu.VMEM((HEADS, ROWS), F32),
            pltpu.VMEM((HEADS, ROWS), F32),
            pltpu.VMEM((HEADS, ROWS), F32),
            pltpu.VMEM((HEADS, ROWS, 128), F32),
            pltpu.VMEM((ROWS, ROWS), F32),
            pltpu.VMEM((ROWS, ROWS), F32),
            pltpu.VMEM((HEADS, ROWS, ROWS), F32),
            pltpu.VMEM((HEADS, ROWS, ROWS), BF16),
            pltpu.VMEM(by_head, F32),
            pltpu.VMEM(by_head, F32),
            pltpu.VMEM(by_head, F32),
            pltpu.VMEM(by_head, F32),
            pltpu.VMEM(by_head, F32),
            pltpu.VMEM(by_head, F32),
            pltpu.VMEM((HEADS, WIDTH, 128), F32),
            pltpu.VMEM(by_head, BF16),
            pltpu.VMEM((STATE, ROWS), BF16),
            pltpu.VMEM((RANKS, HEADS, 128), F32),
            pltpu.VMEM((RANKS, HEADS, 128), F32),
            pltpu.VMEM(by_rank, BF16),
            pltpu.VMEM(by_rank, BF16),
            pltpu.VMEM(by_rank, BF16),
            pltpu.VMEM(by_rank, BF16),
            pltpu.VMEM(by_rank, BF16),
            pltpu.VMEM(by_rank, BF16),
            pltpu.VMEM(by_rank, BF16),
            pltpu.VMEM(by_rank, BF16),
            pltpu.VMEM((2, 2, ROWS, CHANNELS), BF16),
            pltpu.VMEM((4, 1, ROWS), F32),
            pltpu.VMEM((4, 1, ROWS), F32),
            pltpu.VMEM((RING, CHIP_ROWS, 128), F32),
            pltpu.VMEM((RING, CHIP_ROWS, HALF), F32),
            pltpu.VMEM((2, 4, CHIP_ROWS, HALF), BF16),
            pltpu.VMEM((2, 4, CHIP_ROWS, HALF), BF16),
            pltpu.VMEM((CHANNELS, ROWS), F32),
            pltpu.VMEM((CHANNELS, ROWS), F32),
            pltpu.VMEM(by_head, BF16),
            pltpu.VMEM(by_head, BF16),
            pltpu.VMEM((ROWS, ROWS), F32),
            pltpu.VMEM(by_head, F32),
            pltpu.VMEM((HEADS, ROWS), F32),
            pltpu.VMEM((HEADS, ROWS), F32),
            pltpu.VMEM((HEADS, ROWS), F32),
            pltpu.VMEM((HEADS, ROWS), F32),
            pltpu.VMEM((2, 4, WIDTH, ROWS), F32),
            pltpu.VMEM((2, 4, WIDTH, ROWS), BF16),
            pltpu.VMEM((2, 4, WIDTH, ROWS), BF16),
            pltpu.VMEM((2, OWN_ROWS, HALF), BF16),
            pltpu.VMEM((OWN_ROWS, HALF), BF16),
            dma((8,)),
            dma((7,)),
            dma((5,)),
            dma((5,)),
            dma((16,)),
            dma((16,)),
            dma((16,)),
            dma((16,)),
            dma((5, RANKS)),
            dma((5, RANKS)),
            dma((4, 4)),
            dma((4, 4)),
        ],
        compiler_params=pltpu.CompilerParams(
            collective_id=0, has_side_effects=True, vmem_limit_bytes=56 * 1024 * 1024
        ),
        cost_estimate=pl.CostEstimate(
            flops=6_000_000_000, bytes_accessed=16_000_000, transcendentals=1_000_000
        ),
        name="layer",
    )(
        x_in,
        gate_in,
        b_in,
        c_in,
        dt_raw,
        dt_bias,
        a_log,
        skip_weight,
        norm_gain.reshape(1, CHANNELS),
        w_out,
        doc_starts,
        grad_out,
    )
    mixed, grad_x, grad_gate, grad_b, grad_c, grad_dt = pl.pallas_call(
        hand_out,
        out_shape=[jax.ShapeDtypeStruct(o.shape, o.dtype) for o in out],
        in_specs=[vmem] * 6,
        out_specs=[vmem] * 6,
        name="hand_out",
    )(*out)
    return (mixed, grad_x, grad_gate, grad_b.T, grad_c.T, grad_dt)


def solution(mesh):
    return jax.shard_map(
        on_device,
        mesh=mesh,
        in_specs=(
            P("context", "tensor"),
            P("context", "tensor"),
            P("context", None),
            P("context", None),
            P("tensor", "context"),
            P("tensor"),
            P("tensor"),
            P("tensor"),
            P("tensor"),
            P("tensor", None),
            P(),
            P(("context", "tensor"), None),
        ),
        out_specs=(
            P(("context", "tensor"), None),
            P("context", "tensor"),
            P("context", "tensor"),
            P("context", "tensor"),
            P("context", "tensor"),
            P("tensor", "context"),
        ),
        check_vma=False,
    )
```

```python
import jax
import jax.numpy as jnp
from jax import lax
from jax.experimental import pallas as pl
from jax.experimental.pallas import tpu as pltpu
from jax.sharding import PartitionSpec as P

F32 = jnp.float32
BF16 = jnp.bfloat16
HIGH = lax.Precision.HIGHEST
RANKS = 16
SHARDS = 16
RING = 8
HEADS = 8
WIDTH = 64
CHANNELS = HEADS * WIDTH
STATE = 256
ROWS = 256
MODEL = 8192
HALF = MODEL // 2
CHIP_ROWS = ROWS // RING
OWN_ROWS = CHIP_ROWS // 2
PIECE = HALF // 2
CHUNK = CHANNELS // RANKS
TAIL = 16
GROUP_CHANNELS = 2048
EPS = 1e-05


def nn(a, b, precision=None):
    return lax.dot_general(
        a, b, (((1,), (0,)), ((), ())), preferred_element_type=F32, precision=precision
    )


def nt(a, b):
    return lax.dot_general(a, b, (((1,), (1,)), ((), ())), preferred_element_type=F32)


def tn(a, b):
    return lax.dot_general(a, b, (((0,), (0,)), ((), ())), preferred_element_type=F32)


def layer(
    x_hbm,
    gate_hbm,
    b_hbm,
    c_hbm,
    dt_hbm,
    bias_ref,
    alog_ref,
    skip_ref,
    gain_hbm,
    w_hbm,
    docs_ref,
    go_hbm,
    mixed_out,
    gx_out,
    gg_out,
    gb_out,
    gc_out,
    gdt_out,
    x_ref,
    gate_ref,
    dt_ref,
    gain_ref,
    gx_ref,
    gg_ref,
    gb_ref,
    gc_ref,
    gdt_ref,
    bv,
    cv,
    wv,
    gbuf,
    xt,
    r_s,
    e_s,
    wend_s,
    step_s,
    qcol,
    mask,
    gt,
    ws,
    mt,
    yin,
    car,
    yt,
    gated,
    sl,
    dsl,
    gcol,
    wxh,
    cvt,
    keep,
    sb,
    rb,
    eb,
    s0,
    sb2,
    rb2,
    eb2,
    zz,
    gn,
    nbuf,
    abuf,
    fc,
    pp,
    rsend,
    rrecv,
    qsend,
    qrecv,
    dyb,
    edy,
    dgt,
    dxin,
    rowdot,
    coldot,
    cardot,
    zdot,
    gown,
    gsend,
    grecv,
    ob,
    orecv,
    loc,
    out_s,
    pair_s,
    pair_r,
    ag_s,
    ag_r,
    rs_s,
    rs_r,
    ex_s,
    ex_r,
    gr_s,
    gr_r,
):
    rank = lax.axis_index("context")
    shard = lax.axis_index("tensor")
    chip = shard // 2
    core = shard % 2
    other = 1 - core
    group = shard // 4
    member = shard % 4
    sibling = chip * 2 + other
    ahead = ((chip + 1) % RING) * 2 + core
    behind = ((chip + RING - 1) % RING) * 2 + core
    mates = (None, 1 + member - 2 * (member % 2), (member + 2) % 4, 3 - member)

    def remote(src, dst, send, recv, c_to, t_to):
        return pltpu.make_async_remote_copy(
            src_ref=src,
            dst_ref=dst,
            send_sem=send,
            recv_sem=recv,
            device_id=(c_to, t_to),
            device_id_type=pl.DeviceIdType.MESH,
        )

    def each(first, last, body, unroll=1):
        def step(i, carry):
            body(i)
            return carry

        lax.fori_loop(first, last, step, 0, unroll=unroll)

    barrier = pltpu.get_barrier_semaphore()

    def greet(c_to, t_to):
        pl.semaphore_signal(
            barrier, inc=1, device_id=(c_to, t_to), device_id_type=pl.DeviceIdType.MESH
        )

    greet(rank, sibling)
    greet(rank, group * 4 + mates[3])
    greet(rank, ahead)
    greet(rank, behind)
    each(1, RANKS, lambda k: greet((rank + k) % RANKS, shard))

    here = pl.ds(pl.multiple_of(core * HALF, HALF), HALF)
    there = pl.ds(pl.multiple_of(other * HALF, HALF), HALF)
    columns = pl.ds(pl.multiple_of(group * STATE, STATE), STATE)
    load_dt = pltpu.make_async_copy(dt_hbm, dt_ref, loc.at[0])
    load_x = pltpu.make_async_copy(x_hbm, x_ref, loc.at[1])
    load_b = pltpu.make_async_copy(b_hbm.at[:, columns], bv, loc.at[2])
    load_c = pltpu.make_async_copy(c_hbm.at[:, columns], cv, loc.at[3])
    load_gate = pltpu.make_async_copy(gate_hbm, gate_ref, loc.at[4])
    load_gain = pltpu.make_async_copy(gain_hbm, gain_ref, loc.at[5])
    load_go = pltpu.make_async_copy(go_hbm.at[:, here], gbuf.at[chip, core], loc.at[6])
    load_w = pltpu.make_async_copy(w_hbm.at[:, here], wv.at[core], loc.at[7])
    for copy in (load_dt, load_x, load_b, load_c, load_gate, load_gain, load_go, load_w):
        copy.start()

    head_rows = lax.broadcasted_iota(jnp.int32, (HEADS, ROWS), 0)

    def per_head(ref):
        total = jnp.zeros((HEADS, ROWS), F32)
        for h in range(HEADS):
            total = jnp.where(head_rows == h, ref[h], total)
        return total

    load_dt.wait()
    raw = dt_ref[...] + per_head(bias_ref)
    a_rate = -jnp.exp(per_head(alog_ref))
    step = jnp.maximum(raw, 0.0) + jnp.log1p(jnp.exp(-jnp.abs(raw)))
    row_ids = lax.broadcasted_iota(jnp.int32, (ROWS, ROWS), 0)
    col_ids = lax.broadcasted_iota(jnp.int32, (ROWS, ROWS), 1)
    upto = jnp.where(row_ids <= col_ids, 1.0, 0.0)
    running = nn(step * a_rate, upto, HIGH)
    final = running[:, ROWS - 1 : ROWS]
    base = rank * ROWS
    starts = []
    for i in range(4):
        begin = docs_ref[i]
        starts.append(jnp.where(begin >= base, begin - base, 1 << 20))
    pos_row = lax.broadcasted_iota(jnp.int32, (1, ROWS), 1)
    pos_col = lax.broadcasted_iota(jnp.int32, (ROWS, 1), 0)
    seg_row = jnp.zeros((1, ROWS), jnp.int32)
    seg_col = jnp.zeros((ROWS, 1), jnp.int32)
    seg_last = jnp.int32(0)
    for begin in starts:
        seg_row = seg_row + jnp.where(pos_row >= begin, 1, 0)
        seg_col = seg_col + jnp.where(pos_col >= begin, 1, 0)
        seg_last = seg_last + jnp.where(begin <= ROWS - 1, 1, 0)
    opening = seg_row == 0
    closing = seg_row == seg_last
    r_s[...] = running
    step_s[...] = step
    e_s[...] = jnp.where(opening, jnp.exp(running), 0.0)
    wend_s[...] = jnp.where(closing, jnp.exp(final - running), 0.0) * step
    final_hi = final.astype(BF16).astype(F32)
    final_mid = (final - final_hi).astype(BF16).astype(F32)
    final_lo = final - final_hi - final_mid
    tail_rows = lax.broadcasted_iota(jnp.int32, (TAIL, STATE), 0)

    load_x.wait()
    load_b.wait()
    xt[...] = x_ref[...].T.reshape(HEADS, WIDTH, ROWS)
    for h in range(HEADS):
        wx = wend_s[h : h + 1, :] * xt[h].astype(F32)
        wx_hi = wx.astype(BF16)
        wx_lo = (wx - wx_hi.astype(F32)).astype(BF16)
        wxh[h] = wx_hi
        end_state = nn(wx_hi, bv[...]) + nn(wx_lo, bv[...])
        sb[2 * h : 2 * h + 2, :CHUNK] = end_state.astype(BF16).reshape(2, CHUNK, STATE)
        terms = jnp.where(
            tail_rows == 0,
            final_hi[h : h + 1],
            jnp.where(
                tail_rows == 1,
                final_mid[h : h + 1],
                jnp.where(tail_rows == 2, final_lo[h : h + 1], 0.0),
            ),
        ).astype(BF16)
        sb[2 * h, CHUNK:] = terms
        sb[2 * h + 1, CHUNK:] = terms
    rb[rank] = sb[rank]

    pl.semaphore_wait(barrier, 4 + RANKS - 1)
    pair_go = remote(
        go_hbm.at[:, there], gbuf.at[chip, core], pair_s.at[0], pair_r.at[0], rank, sibling
    )
    pair_w = remote(w_hbm.at[:, there], wv.at[core], pair_s.at[1], pair_r.at[1], rank, sibling)

    def spread(which, src, dst):
        def copy(k):
            to = (rank + k) % RANKS
            return remote(
                src.at[to],
                dst.at[rank],
                ex_s.at[which, k],
                ex_r.at[which, k],
                to,
                shard,
            )

        return copy

    ex_state = spread(0, sb, rb)
    ex_enter = spread(1, eb, s0)
    ex_grad = spread(2, sb2, rb2)
    ex_later = spread(3, eb2, zz)

    def ag_copy(hop, way, piece):
        block = (chip + RING - hop) % RING if way == 0 else (chip + hop) % RING
        half = core if piece == 0 else other
        slot = (hop * 2 + way) * 2 + piece
        first = hop == 0 and piece == 0
        return remote(
            go_hbm.at[:, here] if first else gbuf.at[block, half],
            gbuf.at[block, half],
            ag_s.at[slot],
            ag_r.at[slot],
            rank,
            ahead if way == 0 else behind,
        )

    def ag_step(hop, piece):
        for way in range(2):
            if hop < 3 or way == piece:
                if hop:
                    ag_copy(hop - 1, way, piece).wait_recv()
                ag_copy(hop, way, piece).start()

    pair_go.start()
    ag_step(0, 0)
    each(1, RANKS, lambda k: ex_state(k).start())
    pair_w.start()
    pair_go.wait_recv()
    ag_step(0, 1)

    def keep_of(r):
        return keep[r]

    each(1, RANKS, lambda k: ex_state(k).wait_recv())
    for r in range(RANKS):
        count = jnp.int32(0)
        for i in range(4):
            begin = docs_ref[i]
            count = count + jnp.where((begin >= r * ROWS) & (begin < (r + 1) * ROWS), 1, 0)
        whole = jnp.where(count == 0, 1.0, 0.0)
        terms = rb[r, CHUNK:].astype(F32)
        keep[r] = jnp.exp(terms[0:1] + terms[1:2] + terms[2:3]) * whole
    total = jnp.zeros((CHUNK, STATE), F32)
    for r in range(RANKS):
        eb[r] = total.astype(BF16)
        total = keep_of(r) * total + rb[r, :CHUNK].astype(F32)
    each(1, RANKS, lambda k: ex_enter(k).start())
    s0[rank] = eb[rank]

    ag_step(1, 0)
    mask[...] = jnp.where((seg_col == seg_row) & (row_ids <= col_ids), 0.0, -1e30)
    shifted = (running - jnp.log(step)).T
    for h in range(HEADS):
        qcol[h] = jnp.broadcast_to(shifted[:, h : h + 1], (ROWS, 128))

    load_c.wait()
    gt[...] = nt(bv[...], cv[...])

    def inside(h):
        q = qcol[h]
        weight = jnp.exp(r_s[pl.ds(h, 1), :] - jnp.concatenate([q, q], axis=1) + mask[...])
        ws[h] = weight
        mixing = (weight * gt[...]).astype(BF16)
        mt[h] = mixing
        yin[h] = nn(xt[h], mixing)

    each(0, HEADS // 2, inside, 2)
    ag_step(1, 1)
    each(HEADS // 2, HEADS, inside, 2)

    load_gate.wait()
    load_gain.wait()
    v = gate_ref[...].T.astype(F32)
    sig = 1.0 / (1.0 + jnp.exp(-v))
    sl[...] = (v * sig).reshape(HEADS, WIDTH, ROWS)
    dsl[...] = (sig * (1.0 + v * (1.0 - sig))).reshape(HEADS, WIDTH, ROWS)
    eye = row_ids == col_ids
    for q in range(CHANNELS // 128):
        line = gain_ref[:, q * 128 : (q + 1) * 128]
        picked = jnp.where(eye[:128, :128], line, 0.0)
        column = jnp.sum(picked, axis=1, keepdims=True)
        gcol[2 * q : 2 * q + 2] = jnp.broadcast_to(column, (128, 128)).reshape(2, WIDTH, 128)
    cvt[...] = cv[...].T

    each(1, RANKS, lambda k: ex_enter(k).wait_recv())
    ag_step(2, 0)
    enter_all = s0[...].reshape(CHANNELS, STATE)
    car[...] = nt(enter_all, cv[...]).reshape(HEADS, WIDTH, ROWS)

    def finish(h, squares):
        moved = e_s[pl.ds(h, 1), :] * car[h]
        car[h] = moved
        out = yin[h] + moved + skip_ref[h] * xt[h].astype(F32)
        yt[h] = out
        value = out * sl[h]
        gated[h] = value
        return squares + jnp.sum(value * value, axis=0, keepdims=True)

    squares = lax.fori_loop(0, HEADS, finish, jnp.zeros((1, ROWS), F32))
    nbuf[0] = squares

    def mate_copy(which, buf, x):
        return remote(
            buf.at[0],
            buf.at[x],
            gr_s.at[which, x],
            gr_r.at[which, x],
            rank,
            group * 4 + mates[x],
        )

    for x in (1, 2, 3):
        mate_copy(0, nbuf, x).start()
    gain_full = jnp.concatenate([gcol[...], gcol[...]], axis=2)
    scaled = (gated[...] * gain_full).reshape(CHANNELS, ROWS)
    gn[core] = scaled.astype(BF16).T
    pair_gn = remote(gn.at[core], gn.at[core], pair_s.at[2], pair_r.at[2], rank, sibling)
    pair_gn.start()
    ag_step(2, 1)

    load_w.wait()
    pair_w.wait_recv()
    pair_gn.wait_recv()
    tile = 512

    def product(n):
        cols = pl.ds(pl.multiple_of(n * tile, tile), tile)
        value = jnp.zeros((ROWS, tile), F32)
        for one in range(2):
            value = value + nn(gn[one], wv[one, :, cols])
        pp[:, :, cols] = value.reshape(RING, CHIP_ROWS, tile)

    each(0, HALF // tile // 2, product)
    ag_step(3, 0)
    each(HALF // tile // 2, HALF // tile, product)
    ag_step(3, 1)

    for x in (1, 2, 3):
        mate_copy(0, nbuf, x).wait_recv()
    mean = (nbuf[0] + nbuf[1] + nbuf[2] + nbuf[3]) * (1.0 / GROUP_CHANNELS)
    factor = lax.rsqrt(mean + EPS)
    factor_col = jnp.sum(jnp.where(eye, factor, 0.0), axis=1, keepdims=True)
    fc[...] = jnp.broadcast_to(factor_col, (ROWS, 128)).reshape(RING, CHIP_ROWS, 128)

    def own_part(block, piece):
        lanes = fc[block]
        return pp[block, :, piece * PIECE : (piece + 1) * PIECE] * jnp.concatenate(
            [lanes] * (PIECE // 128), axis=1
        )

    def rs_copy(hop, way, piece):
        cols = pl.ds(piece * PIECE, PIECE)
        slot = (hop * 2 + way) * 2 + piece
        return remote(
            rsend.at[way, hop, :, cols],
            rrecv.at[way, hop, :, cols],
            rs_s.at[slot],
            rs_r.at[slot],
            rank,
            ahead if way == 0 else behind,
        )

    def rs_step(hop, turn):
        for way in range(2):
            piece = (way + turn) % 2
            block = (chip + 4 - hop) % RING if way == 0 else (chip + 4 + hop) % RING
            cols = pl.ds(piece * PIECE, PIECE)
            value = own_part(block, piece)
            if hop > turn:
                rs_copy(hop - 1, way, piece).wait_recv()
                value = value + rrecv[way, hop - 1, :, cols].astype(F32)
            rsend[way, hop, :, cols] = value.astype(BF16)
            rs_copy(hop, way, piece).start()

    rs_step(0, 0)

    load_go.wait()
    for way in range(2):
        for piece in range(2):
            ag_copy(3 if way == piece else 2, way, piece).wait_recv()

    def fold(n, total):
        cols = pl.ds(pl.multiple_of(n * tile, tile), tile)
        both = gbuf[:, :, :, cols].reshape(ROWS, tile).astype(F32) * pp[:, :, cols].reshape(
            ROWS, tile
        )
        for i in range(tile // 128):
            total = total + both[:, i * 128 : (i + 1) * 128]
        return total

    along_col = jnp.sum(
        lax.fori_loop(0, HALF // tile, fold, jnp.zeros((ROWS, 128), F32)), axis=1, keepdims=True
    )
    abuf[0] = jnp.sum(jnp.where(eye, along_col, 0.0), axis=0, keepdims=True)
    for x in (1, 2, 3):
        mate_copy(1, abuf, x).start()
    rs_step(1, 1)

    cotangent = gbuf[...].reshape(ROWS, HALF)
    qsend[...] = nt(wv[other], cotangent)
    pair_q = remote(qsend, qrecv, pair_s.at[3], pair_r.at[3], rank, sibling)
    pair_q.start()
    rs_step(1, 0)
    grad_own = nt(wv[core], cotangent)
    pair_q.wait_recv()
    grad_scaled = (grad_own + qrecv[...]).reshape(HEADS, WIDTH, ROWS) * gain_full
    for x in (1, 2, 3):
        mate_copy(1, abuf, x).wait_recv()
    along = abuf[0] + abuf[1] + abuf[2] + abuf[3]
    bend = factor * factor * factor * along * (1.0 / GROUP_CHANNELS)
    grad_gated = grad_scaled * factor[None] - gated[...] * bend[None]
    dy_all = grad_gated * sl[...]
    dyb[...] = dy_all.astype(BF16)
    grad_gate = (grad_gated * yt[...] * dsl[...]).astype(BF16)
    for h in range(HEADS):
        edy[h] = (e_s[h : h + 1, :] * dyb[h].astype(F32)).astype(BF16)
    edy_all = edy[...].reshape(CHANNELS, ROWS)
    sb2[...] = nn(edy_all, cv[...]).astype(BF16).reshape(RANKS, CHUNK, STATE)
    each(1, RANKS, lambda k: ex_grad(k).start())
    rb2[rank] = sb2[rank]
    rs_step(2, 1)
    gg_ref[...] = grad_gate.reshape(CHANNELS, ROWS).T

    def leave(which, source, target):
        return pltpu.make_async_copy(source, target, out_s.at[which])

    leave_gg = leave(0, gg_ref, gg_out)
    leave_gg.start()

    dgt[...] = jnp.zeros((ROWS, ROWS), F32)

    def back(h):
        dy = dyb[h]
        x_now = xt[h]
        dgt[...] += ws[h] * tn(x_now, dy)
        grad_in = nt(dy, mt[h])
        dxin[h] = grad_in
        dyf = dy.astype(F32)
        rowdot[pl.ds(h, 1), :] = jnp.sum(dyf * yin[h], axis=0, keepdims=True)
        cardot[pl.ds(h, 1), :] = jnp.sum(dyf * car[h], axis=0, keepdims=True)
        coldot[pl.ds(h, 1), :] = jnp.sum(x_now.astype(F32) * grad_in, axis=0, keepdims=True)

    each(0, HEADS, back, 2)
    rs_step(2, 0)

    each(1, RANKS, lambda k: ex_grad(k).wait_recv())
    total = jnp.zeros((CHUNK, STATE), F32)
    for r in reversed(range(RANKS)):
        eb2[r] = total.astype(BF16)
        total = keep_of(r) * total + rb2[r].astype(F32)
    each(1, RANKS, lambda k: ex_later(k).start())
    zz[rank] = eb2[rank]
    rs_step(3, 1)

    def share_copy(which, x):
        return remote(
            gsend.at[which, mates[x]],
            grecv.at[which, x],
            gr_s.at[2 + which, x],
            gr_r.at[2 + which, x],
            rank,
            group * 4 + mates[x],
        )

    grad_scores = dgt[...].astype(BF16)
    grad_c = tn(bv[...], grad_scores) + tn(enter_all, edy_all)
    gown[1] = grad_c.reshape(4, WIDTH, ROWS)
    gsend[1] = gown[1].astype(BF16)
    for x in (1, 2, 3):
        share_copy(1, x).start()
    grad_b = nt(cvt[...], grad_scores)
    from_here = jnp.where(row_ids >= col_ids, 1.0, 0.0)
    before = jnp.where(row_ids < col_ids, 1.0, 0.0)
    kept = jnp.where(seg_last == 0, 1.0, 0.0) * jnp.exp(final)
    grad_rate = nn(rowdot[...] - coldot[...] + cardot[...], from_here, HIGH)

    rs_step(3, 0)

    each(1, RANKS, lambda k: ex_later(k).wait_recv())
    later = zz[...].reshape(CHANNELS, STATE)
    grad_b = grad_b + tn(later, wxh[...].reshape(CHANNELS, ROWS))
    gown[0] = grad_b.reshape(4, WIDTH, ROWS)
    gsend[0] = gown[0].astype(BF16)
    for x in (1, 2, 3):
        share_copy(0, x).start()

    moved_back = nt(later, bv[...])
    inner = jnp.zeros((HEADS, ROWS), F32)
    overlap = later.astype(F32) * enter_all.astype(F32)
    for h in range(HEADS):
        part = moved_back[h * WIDTH : (h + 1) * WIDTH, :]
        part = wend_s[h : h + 1, :] * part
        x_now = xt[h].astype(F32)
        zdot[h : h + 1, :] = jnp.sum(x_now * part, axis=0, keepdims=True)
        dxin[h] = dxin[h] + part + skip_ref[h] * dyb[h].astype(F32)
        block = overlap[h * WIDTH : (h + 1) * WIDTH, :]
        inner = jnp.where(head_rows == h, jnp.sum(block), inner)
    gx_ref[...] = dxin[...].reshape(CHANNELS, ROWS).astype(BF16).T
    leave_gx = leave(2, gx_ref, gx_out)
    leave_gx.start()
    grad_rate = grad_rate + nn(zdot[...], before, HIGH) + kept * inner
    grad_step = (coldot[...] + zdot[...]) / step_s[...] + a_rate * grad_rate
    gdt_ref[...] = grad_step * (1.0 / (1.0 + jnp.exp(-raw)))
    leave_dt = leave(3, gdt_ref, gdt_out)
    leave_dt.start()
    for turn in (1, 0):
        for way in range(2):
            rs_copy(3, way, (way + turn) % 2).wait_recv()
    for piece in range(2):
        cols = pl.ds(piece * PIECE, PIECE)
        value = (
            own_part(chip, piece)
            + rrecv[0, 3, :, cols].astype(F32)
            + rrecv[1, 3, :, cols].astype(F32)
        )
        ob[:, :, cols] = value.astype(BF16).reshape(2, OWN_ROWS, PIECE)
    pair_out = remote(ob.at[other], orecv, pair_s.at[4], pair_r.at[4], rank, sibling)
    pair_out.start()
    leave_mine = leave(1, ob.at[core], mixed_out.at[:, here])
    leave_mine.start()

    pair_out.wait_recv()
    leave_theirs = leave(4, orecv, mixed_out.at[:, there])
    leave_theirs.start()

    def gather(which):
        for x in (1, 2, 3):
            share_copy(which, x).wait_recv()
        shares = gown[which, member]
        for x in (1, 2, 3):
            shares = shares + grecv[which, x].astype(F32)
        return shares.astype(BF16)

    gc_ref[...] = gather(1)
    leave_gc = leave(5, gc_ref, gc_out)
    leave_gc.start()
    gb_ref[...] = gather(0)
    leave_gb = leave(6, gb_ref, gb_out)
    leave_gb.start()

    for copy in (pair_go, pair_w, pair_gn, pair_q, pair_out):
        copy.wait_send()
    for hop in range(4):
        for way in range(2):
            for piece in range(2):
                if hop < 3 or way == piece:
                    ag_copy(hop, way, piece).wait_send()
                if hop or way == piece:
                    rs_copy(hop, way, piece).wait_send()
    for exchange in (ex_state, ex_enter, ex_grad, ex_later):
        each(1, RANKS, lambda k: exchange(k).wait_send())
    for x in (1, 2, 3):
        mate_copy(0, nbuf, x).wait_send()
        mate_copy(1, abuf, x).wait_send()
        share_copy(0, x).wait_send()
        share_copy(1, x).wait_send()
    for copy in (leave_gg, leave_mine, leave_gx, leave_dt, leave_theirs, leave_gc, leave_gb):
        copy.wait()


def hand_out(*refs):
    for source, target in zip(refs[:6], refs[6:]):
        target[...] = source[...]


def on_device(
    x_in,
    gate_in,
    b_in,
    c_in,
    dt_raw,
    dt_bias,
    a_log,
    skip_weight,
    norm_gain,
    w_out,
    doc_starts,
    grad_out,
):
    vmem = pl.BlockSpec(memory_space=pltpu.VMEM)
    smem = pl.BlockSpec(memory_space=pltpu.SMEM)
    anywhere = pl.BlockSpec(memory_space=pl.ANY)
    by_head = (HEADS, WIDTH, ROWS)
    by_rank = (RANKS, CHUNK, STATE)
    dma = pltpu.SemaphoreType.DMA
    out = pl.pallas_call(
        layer,
        out_shape=[
            jax.ShapeDtypeStruct((OWN_ROWS, MODEL), BF16),
            jax.ShapeDtypeStruct((ROWS, CHANNELS), BF16),
            jax.ShapeDtypeStruct((ROWS, CHANNELS), BF16),
            jax.ShapeDtypeStruct((WIDTH, ROWS), BF16),
            jax.ShapeDtypeStruct((WIDTH, ROWS), BF16),
            jax.ShapeDtypeStruct((HEADS, ROWS), F32),
        ],
        in_specs=[
            anywhere,
            anywhere,
            anywhere,
            anywhere,
            anywhere,
            smem,
            smem,
            smem,
            anywhere,
            anywhere,
            smem,
            anywhere,
        ],
        out_specs=[anywhere] * 6,
        scratch_shapes=[
            pltpu.VMEM((ROWS, CHANNELS), BF16),
            pltpu.VMEM((ROWS, CHANNELS), BF16),
            pltpu.VMEM((HEADS, ROWS), F32),
            pltpu.VMEM((1, CHANNELS), F32),
            pltpu.VMEM((ROWS, CHANNELS), BF16),
            pltpu.VMEM((ROWS, CHANNELS), BF16),
            pltpu.VMEM((WIDTH, ROWS), BF16),
            pltpu.VMEM((WIDTH, ROWS), BF16),
            pltpu.VMEM((HEADS, ROWS), F32),
            pltpu.VMEM((ROWS, STATE), BF16),
            pltpu.VMEM((ROWS, STATE), BF16),
            pltpu.VMEM((2, CHANNELS, HALF), BF16),
            pltpu.VMEM((RING, 2, OWN_ROWS, HALF), BF16),
            pltpu.VMEM(by_head, BF16),
            pltpu.VMEM((HEADS, ROWS), F32),
            pltpu.VMEM((HEADS, ROWS), F32),
            pltpu.VMEM((HEADS, ROWS), F32),
            pltpu.VMEM((HEADS, ROWS), F32),
            pltpu.VMEM((HEADS, ROWS, 128), F32),
            pltpu.VMEM((ROWS, ROWS), F32),
            pltpu.VMEM((ROWS, ROWS), F32),
            pltpu.VMEM((HEADS, ROWS, ROWS), F32),
            pltpu.VMEM((HEADS, ROWS, ROWS), BF16),
            pltpu.VMEM(by_head, F32),
            pltpu.VMEM(by_head, F32),
            pltpu.VMEM(by_head, F32),
            pltpu.VMEM(by_head, F32),
            pltpu.VMEM(by_head, F32),
            pltpu.VMEM(by_head, F32),
            pltpu.VMEM((HEADS, WIDTH, 128), F32),
            pltpu.VMEM(by_head, BF16),
            pltpu.VMEM((STATE, ROWS), BF16),
            pltpu.VMEM((RANKS, 1, STATE), F32),
            pltpu.VMEM((RANKS, CHUNK + TAIL, STATE), BF16),
            pltpu.VMEM((RANKS, CHUNK + TAIL, STATE), BF16),
            pltpu.VMEM(by_rank, BF16),
            pltpu.VMEM(by_rank, BF16),
            pltpu.VMEM(by_rank, BF16),
            pltpu.VMEM(by_rank, BF16),
            pltpu.VMEM(by_rank, BF16),
            pltpu.VMEM(by_rank, BF16),
            pltpu.VMEM((2, ROWS, CHANNELS), BF16),
            pltpu.VMEM((4, 1, ROWS), F32),
            pltpu.VMEM((4, 1, ROWS), F32),
            pltpu.VMEM((RING, CHIP_ROWS, 128), F32),
            pltpu.VMEM((RING, CHIP_ROWS, HALF), F32),
            pltpu.VMEM((2, 4, CHIP_ROWS, HALF), BF16),
            pltpu.VMEM((2, 4, CHIP_ROWS, HALF), BF16),
            pltpu.VMEM((CHANNELS, ROWS), F32),
            pltpu.VMEM((CHANNELS, ROWS), F32),
            pltpu.VMEM(by_head, BF16),
            pltpu.VMEM(by_head, BF16),
            pltpu.VMEM((ROWS, ROWS), F32),
            pltpu.VMEM(by_head, F32),
            pltpu.VMEM((HEADS, ROWS), F32),
            pltpu.VMEM((HEADS, ROWS), F32),
            pltpu.VMEM((HEADS, ROWS), F32),
            pltpu.VMEM((HEADS, ROWS), F32),
            pltpu.VMEM((2, 4, WIDTH, ROWS), F32),
            pltpu.VMEM((2, 4, WIDTH, ROWS), BF16),
            pltpu.VMEM((2, 4, WIDTH, ROWS), BF16),
            pltpu.VMEM((2, OWN_ROWS, HALF), BF16),
            pltpu.VMEM((OWN_ROWS, HALF), BF16),
            dma((8,)),
            dma((7,)),
            dma((5,)),
            dma((5,)),
            dma((16,)),
            dma((16,)),
            dma((16,)),
            dma((16,)),
            dma((4, RANKS)),
            dma((4, RANKS)),
            dma((4, 4)),
            dma((4, 4)),
        ],
        compiler_params=pltpu.CompilerParams(
            collective_id=0, has_side_effects=True, vmem_limit_bytes=56 * 1024 * 1024
        ),
        cost_estimate=pl.CostEstimate(
            flops=6_000_000_000, bytes_accessed=16_000_000, transcendentals=1_000_000
        ),
        name="layer",
    )(
        x_in,
        gate_in,
        b_in,
        c_in,
        dt_raw,
        dt_bias,
        a_log,
        skip_weight,
        norm_gain.reshape(1, CHANNELS),
        w_out,
        doc_starts,
        grad_out,
    )
    mixed, grad_x, grad_gate, grad_b, grad_c, grad_dt = pl.pallas_call(
        hand_out,
        out_shape=[jax.ShapeDtypeStruct(o.shape, o.dtype) for o in out],
        in_specs=[vmem] * 6,
        out_specs=[vmem] * 6,
        name="hand_out",
    )(*out)
    return (mixed, grad_x, grad_gate, grad_b.T, grad_c.T, grad_dt)


def solution(mesh):
    return jax.shard_map(
        on_device,
        mesh=mesh,
        in_specs=(
            P("context", "tensor"),
            P("context", "tensor"),
            P("context", None),
            P("context", None),
            P("tensor", "context"),
            P("tensor"),
            P("tensor"),
            P("tensor"),
            P("tensor"),
            P("tensor", None),
            P(),
            P(("context", "tensor"), None),
        ),
        out_specs=(
            P(("context", "tensor"), None),
            P("context", "tensor"),
            P("context", "tensor"),
            P("context", "tensor"),
            P("context", "tensor"),
            P("tensor", "context"),
        ),
        check_vma=False,
    )
```

```python
import jax
import jax.numpy as jnp
from jax import lax
from jax.experimental import pallas as pl
from jax.experimental.pallas import tpu as pltpu
from jax.sharding import PartitionSpec as P

F32 = jnp.float32
BF16 = jnp.bfloat16
HIGH = lax.Precision.HIGHEST
RANKS = 16
SHARDS = 16
RING = 8
HEADS = 8
WIDTH = 64
CHANNELS = HEADS * WIDTH
STATE = 256
ROWS = 256
MODEL = 8192
HALF = MODEL // 2
CHIP_ROWS = ROWS // RING
OWN_ROWS = CHIP_ROWS // 2
PIECE = HALF // 2
CHUNK = CHANNELS // RANKS
TAIL = 16
GROUP_CHANNELS = 2048
EPS = 1e-05


def nn(a, b, precision=None):
    return lax.dot_general(
        a, b, (((1,), (0,)), ((), ())), preferred_element_type=F32, precision=precision
    )


def nt(a, b):
    return lax.dot_general(a, b, (((1,), (1,)), ((), ())), preferred_element_type=F32)


def tn(a, b):
    return lax.dot_general(a, b, (((0,), (0,)), ((), ())), preferred_element_type=F32)


def layer(
    x_hbm,
    gate_hbm,
    b_hbm,
    c_hbm,
    dt_hbm,
    bias_ref,
    alog_ref,
    skip_ref,
    gain_hbm,
    w_hbm,
    docs_ref,
    go_hbm,
    mixed_ref,
    gx_ref,
    gg_ref,
    gb_ref,
    gc_ref,
    gdt_ref,
    x_ref,
    gate_ref,
    dt_ref,
    gain_ref,
    bv,
    cv,
    wv,
    gbuf,
    xt,
    r_s,
    e_s,
    wend_s,
    step_s,
    qcol,
    mask,
    gt,
    ws,
    mt,
    yin,
    car,
    yt,
    gated,
    sl,
    dsl,
    gcol,
    wxh,
    cvt,
    keep,
    sb,
    rb,
    eb,
    s0,
    sb2,
    rb2,
    eb2,
    zz,
    sums,
    gn,
    nbuf,
    abuf,
    fc,
    pp,
    rsend,
    rrecv,
    qsend,
    qrecv,
    dyb,
    edy,
    dgt,
    dxin,
    rowdot,
    coldot,
    cardot,
    zdot,
    gown,
    gsend,
    grecv,
    ob,
    orecv,
    loc,
    pair_s,
    pair_r,
    ag_s,
    ag_r,
    rs_s,
    rs_r,
    ex_s,
    ex_r,
    gr_s,
    gr_r,
):
    rank = lax.axis_index("context")
    shard = lax.axis_index("tensor")
    chip = shard // 2
    core = shard % 2
    other = 1 - core
    group = shard // 4
    member = shard % 4
    sibling = chip * 2 + other
    ahead = ((chip + 1) % RING) * 2 + core
    behind = ((chip + RING - 1) % RING) * 2 + core
    mates = (None, 1 + member - 2 * (member % 2), (member + 2) % 4, 3 - member)

    def remote(src, dst, send, recv, c_to, t_to):
        return pltpu.make_async_remote_copy(
            src_ref=src,
            dst_ref=dst,
            send_sem=send,
            recv_sem=recv,
            device_id=(c_to, t_to),
            device_id_type=pl.DeviceIdType.MESH,
        )

    def each(first, last, body, unroll=1):
        def step(i, carry):
            body(i)
            return carry

        lax.fori_loop(first, last, step, 0, unroll=unroll)

    barrier = pltpu.get_barrier_semaphore()

    def greet(c_to, t_to):
        pl.semaphore_signal(
            barrier, inc=1, device_id=(c_to, t_to), device_id_type=pl.DeviceIdType.MESH
        )

    greet(rank, sibling)
    greet(rank, group * 4 + mates[3])
    greet(rank, ahead)
    greet(rank, behind)
    each(1, RANKS, lambda k: greet((rank + k) % RANKS, shard))

    here = pl.ds(pl.multiple_of(core * HALF, HALF), HALF)
    there = pl.ds(pl.multiple_of(other * HALF, HALF), HALF)
    columns = pl.ds(pl.multiple_of(group * STATE, STATE), STATE)
    load_dt = pltpu.make_async_copy(dt_hbm, dt_ref, loc.at[0])
    load_x = pltpu.make_async_copy(x_hbm, x_ref, loc.at[1])
    load_b = pltpu.make_async_copy(b_hbm.at[:, columns], bv, loc.at[2])
    load_c = pltpu.make_async_copy(c_hbm.at[:, columns], cv, loc.at[3])
    load_gate = pltpu.make_async_copy(gate_hbm, gate_ref, loc.at[4])
    load_gain = pltpu.make_async_copy(gain_hbm, gain_ref, loc.at[5])
    load_go = pltpu.make_async_copy(go_hbm.at[:, here], gbuf.at[chip, core], loc.at[6])
    load_w = pltpu.make_async_copy(w_hbm.at[:, here], wv.at[core], loc.at[7])
    for copy in (load_dt, load_x, load_b, load_c, load_gate, load_gain, load_go, load_w):
        copy.start()

    head_rows = lax.broadcasted_iota(jnp.int32, (HEADS, ROWS), 0)

    def per_head(ref):
        total = jnp.zeros((HEADS, ROWS), F32)
        for h in range(HEADS):
            total = jnp.where(head_rows == h, ref[h], total)
        return total

    load_dt.wait()
    raw = dt_ref[...] + per_head(bias_ref)
    a_rate = -jnp.exp(per_head(alog_ref))
    step = jnp.maximum(raw, 0.0) + jnp.log1p(jnp.exp(-jnp.abs(raw)))
    row_ids = lax.broadcasted_iota(jnp.int32, (ROWS, ROWS), 0)
    col_ids = lax.broadcasted_iota(jnp.int32, (ROWS, ROWS), 1)
    upto = jnp.where(row_ids <= col_ids, 1.0, 0.0)
    running = nn(step * a_rate, upto, HIGH)
    final = running[:, ROWS - 1 : ROWS]
    base = rank * ROWS
    starts = []
    for i in range(4):
        begin = docs_ref[i]
        starts.append(jnp.where(begin >= base, begin - base, 1 << 20))
    pos_row = lax.broadcasted_iota(jnp.int32, (1, ROWS), 1)
    pos_col = lax.broadcasted_iota(jnp.int32, (ROWS, 1), 0)
    seg_row = jnp.zeros((1, ROWS), jnp.int32)
    seg_col = jnp.zeros((ROWS, 1), jnp.int32)
    seg_last = jnp.int32(0)
    for begin in starts:
        seg_row = seg_row + jnp.where(pos_row >= begin, 1, 0)
        seg_col = seg_col + jnp.where(pos_col >= begin, 1, 0)
        seg_last = seg_last + jnp.where(begin <= ROWS - 1, 1, 0)
    opening = seg_row == 0
    closing = seg_row == seg_last
    r_s[...] = running
    step_s[...] = step
    e_s[...] = jnp.where(opening, jnp.exp(running), 0.0)
    wend_s[...] = jnp.where(closing, jnp.exp(final - running), 0.0) * step
    final_hi = final.astype(BF16).astype(F32)
    final_mid = (final - final_hi).astype(BF16).astype(F32)
    final_lo = final - final_hi - final_mid
    tail_rows = lax.broadcasted_iota(jnp.int32, (TAIL, STATE), 0)

    load_x.wait()
    load_b.wait()
    xt[...] = x_ref[...].T.reshape(HEADS, WIDTH, ROWS)
    for h in range(HEADS):
        wx = wend_s[h : h + 1, :] * xt[h].astype(F32)
        wx_hi = wx.astype(BF16)
        wx_lo = (wx - wx_hi.astype(F32)).astype(BF16)
        wxh[h] = wx_hi
        end_state = nn(wx_hi, bv[...]) + nn(wx_lo, bv[...])
        sb[2 * h : 2 * h + 2, :CHUNK] = end_state.astype(BF16).reshape(2, CHUNK, STATE)
        terms = jnp.where(
            tail_rows == 0,
            final_hi[h : h + 1],
            jnp.where(
                tail_rows == 1,
                final_mid[h : h + 1],
                jnp.where(tail_rows == 2, final_lo[h : h + 1], 0.0),
            ),
        ).astype(BF16)
        sb[2 * h, CHUNK:] = terms
        sb[2 * h + 1, CHUNK:] = terms
    rb[rank] = sb[rank]

    pl.semaphore_wait(barrier, 4 + RANKS - 1)
    pair_go = remote(
        go_hbm.at[:, there], gbuf.at[chip, core], pair_s.at[0], pair_r.at[0], rank, sibling
    )
    pair_w = remote(w_hbm.at[:, there], wv.at[core], pair_s.at[1], pair_r.at[1], rank, sibling)

    def spread(which, src, dst):
        def copy(k):
            to = (rank + k) % RANKS
            return remote(
                src.at[to],
                dst.at[rank],
                ex_s.at[which, k],
                ex_r.at[which, k],
                to,
                shard,
            )

        return copy

    ex_state = spread(0, sb, rb)
    ex_enter = spread(1, eb, s0)
    ex_grad = spread(2, sb2, rb2)
    ex_later = spread(3, eb2, zz)

    def ag_copy(hop, way, piece):
        block = (chip + RING - hop) % RING if way == 0 else (chip + hop) % RING
        half = core if piece == 0 else other
        slot = (hop * 2 + way) * 2 + piece
        first = hop == 0 and piece == 0
        return remote(
            go_hbm.at[:, here] if first else gbuf.at[block, half],
            gbuf.at[block, half],
            ag_s.at[slot],
            ag_r.at[slot],
            rank,
            ahead if way == 0 else behind,
        )

    def ag_step(hop, piece):
        for way in range(2):
            if hop < 3 or way == piece:
                if hop:
                    ag_copy(hop - 1, way, piece).wait_recv()
                ag_copy(hop, way, piece).start()

    pair_go.start()
    ag_step(0, 0)
    each(1, RANKS, lambda k: ex_state(k).start())
    pair_w.start()
    pair_go.wait_recv()
    ag_step(0, 1)

    def keep_of(r):
        return keep[r]

    ag_step(1, 0)
    each(1, RANKS, lambda k: ex_state(k).wait_recv())
    for r in range(RANKS):
        count = jnp.int32(0)
        for i in range(4):
            begin = docs_ref[i]
            count = count + jnp.where((begin >= r * ROWS) & (begin < (r + 1) * ROWS), 1, 0)
        whole = jnp.where(count == 0, 1.0, 0.0)
        terms = rb[r, CHUNK:].astype(F32)
        keep[r] = jnp.exp(terms[0:1] + terms[1:2] + terms[2:3]) * whole
    total = jnp.zeros((CHUNK, STATE), F32)
    for r in range(RANKS):
        eb[r] = total.astype(BF16)
        total = keep_of(r) * total + rb[r, :CHUNK].astype(F32)
    each(1, RANKS, lambda k: ex_enter(k).start())
    s0[rank] = eb[rank]

    mask[...] = jnp.where((seg_col == seg_row) & (row_ids <= col_ids), 0.0, -1e30)
    shifted = (running - jnp.log(step)).T
    for h in range(HEADS):
        qcol[h] = jnp.broadcast_to(shifted[:, h : h + 1], (ROWS, 128))

    load_c.wait()
    gt[...] = nt(bv[...], cv[...])

    def inside(h):
        q = qcol[h]
        weight = jnp.exp(r_s[pl.ds(h, 1), :] - jnp.concatenate([q, q], axis=1) + mask[...])
        ws[h] = weight
        mixing = (weight * gt[...]).astype(BF16)
        mt[h] = mixing
        yin[h] = nn(xt[h], mixing)

    each(0, HEADS // 2, inside, 2)
    ag_step(1, 1)
    each(HEADS // 2, HEADS, inside, 2)

    load_gate.wait()
    load_gain.wait()
    v = gate_ref[...].T.astype(F32)
    sig = 1.0 / (1.0 + jnp.exp(-v))
    sl[...] = (v * sig).reshape(HEADS, WIDTH, ROWS)
    dsl[...] = (sig * (1.0 + v * (1.0 - sig))).reshape(HEADS, WIDTH, ROWS)
    eye = row_ids == col_ids
    for q in range(CHANNELS // 128):
        line = gain_ref[:, q * 128 : (q + 1) * 128]
        picked = jnp.where(eye[:128, :128], line, 0.0)
        column = jnp.sum(picked, axis=1, keepdims=True)
        gcol[2 * q : 2 * q + 2] = jnp.broadcast_to(column, (128, 128)).reshape(2, WIDTH, 128)
    cvt[...] = cv[...].T

    ag_step(2, 0)

    each(1, RANKS, lambda k: ex_enter(k).wait_recv())
    enter_all = s0[...].reshape(CHANNELS, STATE)
    car[...] = nt(enter_all, cv[...]).reshape(HEADS, WIDTH, ROWS)

    def finish(h, squares):
        moved = e_s[pl.ds(h, 1), :] * car[h]
        car[h] = moved
        out = yin[h] + moved + skip_ref[h] * xt[h].astype(F32)
        yt[h] = out
        value = out * sl[h]
        gated[h] = value
        return squares + jnp.sum(value * value, axis=0, keepdims=True)

    squares = lax.fori_loop(0, HEADS, finish, jnp.zeros((1, ROWS), F32))
    nbuf[0] = squares

    def mate_copy(which, buf, x):
        return remote(
            buf.at[0],
            buf.at[x],
            gr_s.at[which, x],
            gr_r.at[which, x],
            rank,
            group * 4 + mates[x],
        )

    for x in (1, 2, 3):
        mate_copy(0, nbuf, x).start()
    gain_full = jnp.concatenate([gcol[...], gcol[...]], axis=2)
    scaled = (gated[...] * gain_full).reshape(CHANNELS, ROWS)
    gn[core] = scaled.astype(BF16).T
    pair_gn = remote(gn.at[core], gn.at[core], pair_s.at[2], pair_r.at[2], rank, sibling)
    pair_gn.start()
    ag_step(2, 1)

    load_w.wait()
    pair_w.wait_recv()
    pair_gn.wait_recv()
    tile = 512

    def product(n):
        cols = pl.ds(pl.multiple_of(n * tile, tile), tile)
        value = jnp.zeros((ROWS, tile), F32)
        for one in range(2):
            value = value + nn(gn[one], wv[one, :, cols])
        pp[:, :, cols] = value.reshape(RING, CHIP_ROWS, tile)

    each(0, HALF // tile // 2, product)
    ag_step(3, 0)
    each(HALF // tile // 2, HALF // tile, product)
    ag_step(3, 1)

    for x in (1, 2, 3):
        mate_copy(0, nbuf, x).wait_recv()
    mean = (nbuf[0] + nbuf[1] + nbuf[2] + nbuf[3]) * (1.0 / GROUP_CHANNELS)
    factor = lax.rsqrt(mean + EPS)
    factor_col = jnp.sum(jnp.where(eye, factor, 0.0), axis=1, keepdims=True)
    fc[...] = jnp.broadcast_to(factor_col, (ROWS, 128)).reshape(RING, CHIP_ROWS, 128)

    def own_part(block, piece):
        lanes = fc[block]
        return pp[block, :, piece * PIECE : (piece + 1) * PIECE] * jnp.concatenate(
            [lanes] * (PIECE // 128), axis=1
        )

    def rs_copy(hop, way, piece):
        cols = pl.ds(piece * PIECE, PIECE)
        slot = (hop * 2 + way) * 2 + piece
        return remote(
            rsend.at[way, hop, :, cols],
            rrecv.at[way, hop, :, cols],
            rs_s.at[slot],
            rs_r.at[slot],
            rank,
            ahead if way == 0 else behind,
        )

    def rs_step(hop, turn):
        for way in range(2):
            piece = (way + turn) % 2
            block = (chip + 4 - hop) % RING if way == 0 else (chip + 4 + hop) % RING
            cols = pl.ds(piece * PIECE, PIECE)
            value = own_part(block, piece)
            if hop > turn:
                rs_copy(hop - 1, way, piece).wait_recv()
                value = value + rrecv[way, hop - 1, :, cols].astype(F32)
            rsend[way, hop, :, cols] = value.astype(BF16)
            rs_copy(hop, way, piece).start()

    rs_step(0, 0)

    load_go.wait()

    def fold(block):
        total = jnp.zeros((CHIP_ROWS, 128), F32)
        for n in range(HALF // tile):
            cols = pl.ds(n * tile, tile)
            part = gbuf[block, :, :, cols].reshape(CHIP_ROWS, tile).astype(F32)
            both = part * pp[block, :, cols]
            for i in range(tile // 128):
                total = total + both[:, i * 128 : (i + 1) * 128]
        sums[block] = total

    def fold_far(d):
        fold((chip + d) % RING)

    each(0, 3, fold_far)
    each(RING - 2, RING, fold_far)
    for way in range(2):
        for piece in range(2):
            ag_copy(3 if way == piece else 2, way, piece).wait_recv()
    each(3, 6, fold_far)
    along_col = jnp.sum(sums[...].reshape(ROWS, 128), axis=1, keepdims=True)
    abuf[0] = jnp.sum(jnp.where(eye, along_col, 0.0), axis=0, keepdims=True)
    for x in (1, 2, 3):
        mate_copy(1, abuf, x).start()
    rs_step(1, 1)

    cotangent = gbuf[...].reshape(ROWS, HALF)
    qsend[...] = nt(wv[other], cotangent)
    pair_q = remote(qsend, qrecv, pair_s.at[3], pair_r.at[3], rank, sibling)
    pair_q.start()
    grad_own = nt(wv[core], cotangent)
    rs_step(1, 0)
    pair_q.wait_recv()
    grad_scaled = (grad_own + qrecv[...]).reshape(HEADS, WIDTH, ROWS) * gain_full
    for x in (1, 2, 3):
        mate_copy(1, abuf, x).wait_recv()
    along = abuf[0] + abuf[1] + abuf[2] + abuf[3]
    bend = factor * factor * factor * along * (1.0 / GROUP_CHANNELS)
    grad_gated = grad_scaled * factor[None] - gated[...] * bend[None]
    dy_all = grad_gated * sl[...]
    dyb[...] = dy_all.astype(BF16)
    grad_gate = (grad_gated * yt[...] * dsl[...]).astype(BF16)
    for h in range(HEADS):
        edy[h] = (e_s[h : h + 1, :] * dyb[h].astype(F32)).astype(BF16)
    edy_all = edy[...].reshape(CHANNELS, ROWS)
    sb2[...] = nn(edy_all, cv[...]).astype(BF16).reshape(RANKS, CHUNK, STATE)
    each(1, RANKS, lambda k: ex_grad(k).start())
    rb2[rank] = sb2[rank]
    rs_step(2, 1)
    gg_ref[...] = grad_gate.reshape(CHANNELS, ROWS).T


    dgt[...] = jnp.zeros((ROWS, ROWS), F32)

    def back(h):
        dy = dyb[h]
        x_now = xt[h]
        dgt[...] += ws[h] * tn(x_now, dy)
        grad_in = nt(dy, mt[h])
        dxin[h] = grad_in
        dyf = dy.astype(F32)
        rowdot[pl.ds(h, 1), :] = jnp.sum(dyf * yin[h], axis=0, keepdims=True)
        cardot[pl.ds(h, 1), :] = jnp.sum(dyf * car[h], axis=0, keepdims=True)
        coldot[pl.ds(h, 1), :] = jnp.sum(x_now.astype(F32) * grad_in, axis=0, keepdims=True)

    each(0, HEADS, back, 2)
    rs_step(2, 0)

    each(1, RANKS, lambda k: ex_grad(k).wait_recv())
    total = jnp.zeros((CHUNK, STATE), F32)
    for r in reversed(range(RANKS)):
        eb2[r] = total.astype(BF16)
        total = keep_of(r) * total + rb2[r].astype(F32)
    each(1, RANKS, lambda k: ex_later(k).start())
    zz[rank] = eb2[rank]
    rs_step(3, 1)

    def share_copy(which, x):
        return remote(
            gsend.at[which, mates[x]],
            grecv.at[which, x],
            gr_s.at[2 + which, x],
            gr_r.at[2 + which, x],
            rank,
            group * 4 + mates[x],
        )

    grad_scores = dgt[...].astype(BF16)
    grad_c = tn(bv[...], grad_scores) + tn(enter_all, edy_all)
    gown[1] = grad_c.reshape(4, WIDTH, ROWS)
    gsend[1] = gown[1].astype(BF16)
    for x in (1, 2, 3):
        share_copy(1, x).start()
    grad_b = nt(cvt[...], grad_scores)
    from_here = jnp.where(row_ids >= col_ids, 1.0, 0.0)
    before = jnp.where(row_ids < col_ids, 1.0, 0.0)
    kept = jnp.where(seg_last == 0, 1.0, 0.0) * jnp.exp(final)
    grad_rate = nn(rowdot[...] - coldot[...] + cardot[...], from_here, HIGH)

    rs_step(3, 0)

    each(1, RANKS, lambda k: ex_later(k).wait_recv())
    later = zz[...].reshape(CHANNELS, STATE)
    grad_b = grad_b + tn(later, wxh[...].reshape(CHANNELS, ROWS))
    gown[0] = grad_b.reshape(4, WIDTH, ROWS)
    gsend[0] = gown[0].astype(BF16)
    for x in (1, 2, 3):
        share_copy(0, x).start()

    moved_back = nt(later, bv[...])
    inner = jnp.zeros((HEADS, ROWS), F32)
    overlap = later.astype(F32) * enter_all.astype(F32)
    for h in range(HEADS):
        part = moved_back[h * WIDTH : (h + 1) * WIDTH, :]
        part = wend_s[h : h + 1, :] * part
        x_now = xt[h].astype(F32)
        zdot[h : h + 1, :] = jnp.sum(x_now * part, axis=0, keepdims=True)
        dxin[h] = dxin[h] + part + skip_ref[h] * dyb[h].astype(F32)
        block = overlap[h * WIDTH : (h + 1) * WIDTH, :]
        inner = jnp.where(head_rows == h, jnp.sum(block), inner)
    gx_ref[...] = dxin[...].reshape(CHANNELS, ROWS).astype(BF16).T
    grad_rate = grad_rate + nn(zdot[...], before, HIGH) + kept * inner
    grad_step = (coldot[...] + zdot[...]) / step_s[...] + a_rate * grad_rate
    gdt_ref[...] = grad_step * (1.0 / (1.0 + jnp.exp(-raw)))
    for turn in (1, 0):
        for way in range(2):
            rs_copy(3, way, (way + turn) % 2).wait_recv()
    for piece in range(2):
        cols = pl.ds(piece * PIECE, PIECE)
        value = (
            own_part(chip, piece)
            + rrecv[0, 3, :, cols].astype(F32)
            + rrecv[1, 3, :, cols].astype(F32)
        )
        ob[:, :, cols] = value.astype(BF16).reshape(2, OWN_ROWS, PIECE)
    pair_out = remote(ob.at[other], orecv, pair_s.at[4], pair_r.at[4], rank, sibling)
    pair_out.start()
    mixed_ref[:, here] = ob[core]

    pair_out.wait_recv()
    mixed_ref[:, there] = orecv[...]

    def gather(which):
        for x in (1, 2, 3):
            share_copy(which, x).wait_recv()
        shares = gown[which, member]
        for x in (1, 2, 3):
            shares = shares + grecv[which, x].astype(F32)
        return shares.astype(BF16)

    gc_ref[...] = gather(1)
    gb_ref[...] = gather(0)

    for copy in (pair_go, pair_w, pair_gn, pair_q, pair_out):
        copy.wait_send()
    for hop in range(4):
        for way in range(2):
            for piece in range(2):
                if hop < 3 or way == piece:
                    ag_copy(hop, way, piece).wait_send()
                if hop or way == piece:
                    rs_copy(hop, way, piece).wait_send()
    for exchange in (ex_state, ex_enter, ex_grad, ex_later):
        each(1, RANKS, lambda k: exchange(k).wait_send())
    for x in (1, 2, 3):
        mate_copy(0, nbuf, x).wait_send()
        mate_copy(1, abuf, x).wait_send()
        share_copy(0, x).wait_send()
        share_copy(1, x).wait_send()


def hand_out(*refs):
    for source, target in zip(refs[:6], refs[6:]):
        target[...] = source[...]


def on_device(
    x_in,
    gate_in,
    b_in,
    c_in,
    dt_raw,
    dt_bias,
    a_log,
    skip_weight,
    norm_gain,
    w_out,
    doc_starts,
    grad_out,
):
    vmem = pl.BlockSpec(memory_space=pltpu.VMEM)
    smem = pl.BlockSpec(memory_space=pltpu.SMEM)
    anywhere = pl.BlockSpec(memory_space=pl.ANY)
    by_head = (HEADS, WIDTH, ROWS)
    by_rank = (RANKS, CHUNK, STATE)
    dma = pltpu.SemaphoreType.DMA
    out = pl.pallas_call(
        layer,
        out_shape=[
            pltpu.VMEM((OWN_ROWS, MODEL), BF16),
            pltpu.VMEM((ROWS, CHANNELS), BF16),
            pltpu.VMEM((ROWS, CHANNELS), BF16),
            pltpu.VMEM((WIDTH, ROWS), BF16),
            pltpu.VMEM((WIDTH, ROWS), BF16),
            pltpu.VMEM((HEADS, ROWS), F32),
        ],
        in_specs=[
            anywhere,
            anywhere,
            anywhere,
            anywhere,
            anywhere,
            smem,
            smem,
            smem,
            anywhere,
            anywhere,
            smem,
            anywhere,
        ],
        out_specs=[vmem] * 6,
        scratch_shapes=[
            pltpu.VMEM((ROWS, CHANNELS), BF16),
            pltpu.VMEM((ROWS, CHANNELS), BF16),
            pltpu.VMEM((HEADS, ROWS), F32),
            pltpu.VMEM((1, CHANNELS), F32),
            pltpu.VMEM((ROWS, STATE), BF16),
            pltpu.VMEM((ROWS, STATE), BF16),
            pltpu.VMEM((2, CHANNELS, HALF), BF16),
            pltpu.VMEM((RING, 2, OWN_ROWS, HALF), BF16),
            pltpu.VMEM(by_head, BF16),
            pltpu.VMEM((HEADS, ROWS), F32),
            pltpu.VMEM((HEADS, ROWS), F32),
            pltpu.VMEM((HEADS, ROWS), F32),
            pltpu.VMEM((HEADS, ROWS), F32),
            pltpu.VMEM((HEADS, ROWS, 128), F32),
            pltpu.VMEM((ROWS, ROWS), F32),
            pltpu.VMEM((ROWS, ROWS), F32),
            pltpu.VMEM((HEADS, ROWS, ROWS), F32),
            pltpu.VMEM((HEADS, ROWS, ROWS), BF16),
            pltpu.VMEM(by_head, F32),
            pltpu.VMEM(by_head, F32),
            pltpu.VMEM(by_head, F32),
            pltpu.VMEM(by_head, F32),
            pltpu.VMEM(by_head, F32),
            pltpu.VMEM(by_head, F32),
            pltpu.VMEM((HEADS, WIDTH, 128), F32),
            pltpu.VMEM(by_head, BF16),
            pltpu.VMEM((STATE, ROWS), BF16),
            pltpu.VMEM((RANKS, 1, STATE), F32),
            pltpu.VMEM((RANKS, CHUNK + TAIL, STATE), BF16),
            pltpu.VMEM((RANKS, CHUNK + TAIL, STATE), BF16),
            pltpu.VMEM(by_rank, BF16),
            pltpu.VMEM(by_rank, BF16),
            pltpu.VMEM(by_rank, BF16),
            pltpu.VMEM(by_rank, BF16),
            pltpu.VMEM(by_rank, BF16),
            pltpu.VMEM(by_rank, BF16),
            pltpu.VMEM((RING, CHIP_ROWS, 128), F32),
            pltpu.VMEM((2, ROWS, CHANNELS), BF16),
            pltpu.VMEM((4, 1, ROWS), F32),
            pltpu.VMEM((4, 1, ROWS), F32),
            pltpu.VMEM((RING, CHIP_ROWS, 128), F32),
            pltpu.VMEM((RING, CHIP_ROWS, HALF), F32),
            pltpu.VMEM((2, 4, CHIP_ROWS, HALF), BF16),
            pltpu.VMEM((2, 4, CHIP_ROWS, HALF), BF16),
            pltpu.VMEM((CHANNELS, ROWS), F32),
            pltpu.VMEM((CHANNELS, ROWS), F32),
            pltpu.VMEM(by_head, BF16),
            pltpu.VMEM(by_head, BF16),
            pltpu.VMEM((ROWS, ROWS), F32),
            pltpu.VMEM(by_head, F32),
            pltpu.VMEM((HEADS, ROWS), F32),
            pltpu.VMEM((HEADS, ROWS), F32),
            pltpu.VMEM((HEADS, ROWS), F32),
            pltpu.VMEM((HEADS, ROWS), F32),
            pltpu.VMEM((2, 4, WIDTH, ROWS), F32),
            pltpu.VMEM((2, 4, WIDTH, ROWS), BF16),
            pltpu.VMEM((2, 4, WIDTH, ROWS), BF16),
            pltpu.VMEM((2, OWN_ROWS, HALF), BF16),
            pltpu.VMEM((OWN_ROWS, HALF), BF16),
            dma((8,)),
            dma((5,)),
            dma((5,)),
            dma((16,)),
            dma((16,)),
            dma((16,)),
            dma((16,)),
            dma((4, RANKS)),
            dma((4, RANKS)),
            dma((4, 4)),
            dma((4, 4)),
        ],
        compiler_params=pltpu.CompilerParams(
            collective_id=0, has_side_effects=True, vmem_limit_bytes=56 * 1024 * 1024
        ),
        cost_estimate=pl.CostEstimate(
            flops=6_000_000_000, bytes_accessed=16_000_000, transcendentals=1_000_000
        ),
        name="layer",
    )(
        x_in,
        gate_in,
        b_in,
        c_in,
        dt_raw,
        dt_bias,
        a_log,
        skip_weight,
        norm_gain.reshape(1, CHANNELS),
        w_out,
        doc_starts,
        grad_out,
    )
    mixed, grad_x, grad_gate, grad_b, grad_c, grad_dt = pl.pallas_call(
        hand_out,
        out_shape=[jax.ShapeDtypeStruct(o.shape, o.dtype) for o in out],
        in_specs=[vmem] * 6,
        out_specs=[vmem] * 6,
        compiler_params=pltpu.CompilerParams(vmem_limit_bytes=4 * 1024 * 1024),
        name="hand_out",
    )(*out)
    return (mixed, grad_x, grad_gate, grad_b.T, grad_c.T, grad_dt)


def solution(mesh):
    return jax.shard_map(
        on_device,
        mesh=mesh,
        in_specs=(
            P("context", "tensor"),
            P("context", "tensor"),
            P("context", None),
            P("context", None),
            P("tensor", "context"),
            P("tensor"),
            P("tensor"),
            P("tensor"),
            P("tensor"),
            P("tensor", None),
            P(),
            P(("context", "tensor"), None),
        ),
        out_specs=(
            P(("context", "tensor"), None),
            P("context", "tensor"),
            P("context", "tensor"),
            P("context", "tensor"),
            P("context", "tensor"),
            P("tensor", "context"),
        ),
        check_vma=False,
    )
```
